128 devices in a mesh: ctx: 32 (over x, y, core), wt: 4 (over z).
Axes of the slice: x: 4, y: 4, z: 4, core: 2. Of those that a mesh axis runs over, the one named last changes fastest.
Arguments:
- tokens_in: bfloat16 [8, 2, 1024, 768], P('wt', None, 'ctx'), may hold values from -6 to 6
- cotangent: bfloat16 [8, 2, 1024, 768], P('wt', None, 'ctx'), may hold values from -6 to 6
- ln_gain_attn: bfloat16 [2, 768], P(None, 'wt'), may hold values from 0.5 to 1.5
- ln_shift_attn: bfloat16 [2, 768], P(None, 'wt'), may hold values from -1.5 to 1.5
- ln_gain_mlp: bfloat16 [2, 768], P(None, 'wt'), may hold values from 0.5 to 1.5
- ln_shift_mlp: bfloat16 [2, 768], P(None, 'wt'), may hold values from -1.5 to 1.5
- w_qkv: bfloat16 [2, 768, 2304], P(None, 'wt'), may hold values from -0.21875 to 0.21875
- b_qv: bfloat16 [2, 1536], P(None, 'wt'), may hold values from -2.5 to 2.5
- w_out: bfloat16 [2, 768, 768], P(None, 'wt'), may hold values from -6 to 6
- b_out: bfloat16 [2, 768], P(None, 'wt'), may hold values from -1.5 to 1.5
- w_up: bfloat16 [2, 768, 3072], P(None, 'wt'), may hold values from -0.21875 to 0.21875
- b_up: bfloat16 [2, 3072], P(None, 'wt'), may hold values from -2.5 to 2.5
- w_down: bfloat16 [2, 3072, 768], P(None, 'wt'), may hold values from -0.109375 to 0.109375
- b_down: bfloat16 [2, 768], P(None, 'wt'), may hold values from -1.5 to 1.5
Outputs:
- out_tokens: bfloat16 [8, 2, 1024, 768], P('wt', None, 'ctx')
- grad_tokens: float32 [8, 2, 1024, 768], P('wt', None, 'ctx')
- grad_ln_gain_attn: float32 [2, 768], P(None, 'wt')
- grad_ln_shift_attn: float32 [2, 768], P(None, 'wt')
- grad_ln_gain_mlp: float32 [2, 768], P(None, 'wt')
- grad_ln_shift_mlp: float32 [2, 768], P(None, 'wt')
- grad_w_qkv: float32 [2, 768, 2304], P(None, 'wt')
- grad_b_qv: float32 [2, 1536], P(None, 'wt')
- grad_w_out: float32 [2, 768, 768], P(None, 'wt')
- grad_b_out: float32 [2, 768], P(None, 'wt')
- grad_w_up: float32 [2, 768, 3072], P(None, 'wt')
- grad_b_up: float32 [2, 3072], P(None, 'wt')
- grad_w_down: float32 [2, 3072, 768], P(None, 'wt')
- grad_b_down: float32 [2, 768], P(None, 'wt')
The draws below stay inside these ranges and needn't reach their ends.
All inputs are finite; a program needn't handle non-finite values.
Results may differ from the reference program's by a relative error of at most 0.02.
Values may be sent and summed in bfloat16 or wider, within the bound.
No kernel may reach another device: no remote copies, remote signals or barrier semaphores. Data moves between devices by JAX's collectives and lax.ppermute only.
A program may use at most 256 MiB of HBM per device.

```python
import jax
import jax.numpy as jnp
from jax import lax

D = 768
FF = 3072
HEADS = 12
HEAD_DIM = 64
ROT = 16
LAYERS = 2
BLK = 32
HALF = 1024
SEQ_LEN = 2048
SEQS = 8
N_CTX = 32


def steps_of(own_key, shape, cuts, low, top_value):
    def one(axis_at, parts):
        steps = jax.random.uniform(jax.random.fold_in(jax.random.fold_in(own_key, 6), axis_at), (parts,), jnp.float32, low / len(cuts), top_value / len(cuts))
        return jnp.repeat(jnp.exp(steps), shape[axis_at] // parts).reshape((-1,) + (1,) * (len(shape) - axis_at - 1))

    level = one(*cuts[0])
    for cut in cuts[1:]:
        level = level * one(*cut)
    return level


def normal_values(stream_key, extent, scale, limit, cuts=(), held_as=jnp.bfloat16):
    values = scale * jax.random.normal(stream_key, extent, jnp.float32)
    if cuts:
        values = values * steps_of(stream_key, extent, cuts, -0.22, 0.18)
    return jnp.clip(values, -limit, limit).astype(held_as)


def setup_inputs(seed: int = 0) -> dict:
    arg_keys = jax.random.split(jax.random.key(seed), 15)
    return {
        "tokens_in": normal_values(arg_keys[0], (SEQS, 2, HALF, D), 1.0, 6.0, ((0, 4), (2, 32))),
        "cotangent": normal_values(arg_keys[1], (SEQS, 2, HALF, D), 1.0, 6.0, ((0, 4), (2, 32))),
        "ln_gain_attn": jnp.clip(1.0 + 0.1 * jax.random.normal(arg_keys[2], (LAYERS, D), jnp.float32), 0.5, 1.5).astype(jnp.bfloat16),
        "ln_shift_attn": normal_values(arg_keys[3], (LAYERS, D), 0.3, 1.5, ((1, 4),)),
        "ln_gain_mlp": jnp.clip(1.0 + 0.1 * jax.random.normal(arg_keys[4], (LAYERS, D), jnp.float32), 0.5, 1.5).astype(jnp.bfloat16),
        "ln_shift_mlp": normal_values(arg_keys[5], (LAYERS, D), 0.3, 1.5, ((1, 4),)),
        "w_qkv": normal_values(arg_keys[6], (LAYERS, D, 3 * D), D ** -0.5, 0.21875, ((1, 4),)),
        "b_qv": normal_values(arg_keys[7], (LAYERS, 2 * D), 0.5, 2.5, ((1, 4),)),
        "w_out": normal_values(arg_keys[8], (LAYERS, D, D), (max(1, 2 * D // SEQ_LEN)) ** -0.5, 6.0, ((1, 4),)),
        "b_out": normal_values(arg_keys[9], (LAYERS, D), 0.3, 1.5, ((1, 4),)),
        "w_up": normal_values(arg_keys[10], (LAYERS, D, FF), D ** -0.5, 0.21875, ((1, 4),)),
        "b_up": normal_values(arg_keys[11], (LAYERS, FF), 0.5, 2.5, ((1, 4),)),
        "w_down": normal_values(arg_keys[12], (LAYERS, FF, D), FF ** -0.5, 0.109375, ((1, 4),)),
        "b_down": normal_values(arg_keys[13], (LAYERS, D), 0.3, 1.5, ((1, 4),)),
    }


norm_epsilon = 1e-05

@jax.custom_vjp
def low(v):
    return lax.optimization_barrier(v.astype(jnp.bfloat16)).astype(jnp.float32)

@jax.custom_vjp
def low_back(v):
    return v

def low_keep(v):
    return (low(v), None)

def low_pass(kept, grad):
    return (grad,)

def back_keep(v):
    return (v, None)

def back_low(kept, grad):
    return (low(grad),)
low.defvjp(low_keep, low_pass)
low_back.defvjp(back_keep, back_low)

def high_dot(left, right):
    return jnp.dot(left, right, precision=lax.Precision.HIGHEST)

def normalize(values, gain, shift):
    centre = lax.optimization_barrier(jnp.mean(values, axis=-1, keepdims=True))
    centred = values - centre
    spread = lax.optimization_barrier(jnp.mean(centred * centred, axis=-1, keepdims=True))
    return centred * lax.rsqrt(spread + norm_epsilon) * gain + shift

def rotate(values, positions):
    halfway = ROT // 2
    frequency = 10000.0 ** (-jnp.arange(halfway, dtype=jnp.float32) * 2.0 / ROT)
    angles = positions.astype(jnp.float32)[:, None] * frequency[None, :]
    cosine = jnp.cos(angles)[:, None, :]
    sine_part = jnp.sin(angles)[:, None, :]
    leading = values[..., :halfway]
    trailing = values[..., halfway:ROT]
    return jnp.concatenate([leading * cosine - trailing * sine_part, trailing * cosine + leading * sine_part, values[..., ROT:]], axis=-1)

def attend(queries, keys_all, values_all):
    block = min(512, SEQ_LEN)
    count = SEQ_LEN // block
    scaling = HEAD_DIM ** (-0.5)
    key_positions = jnp.arange(SEQ_LEN, dtype=jnp.int32)

    def one_block(item):
        sequence = (item // count).astype(jnp.int32)
        start = (item % count * block).astype(jnp.int32)
        seq_queries = lax.dynamic_index_in_dim(queries, sequence, 0, keepdims=False)
        block_queries = lax.dynamic_slice_in_dim(seq_queries, start, block, 0)
        seq_keys = lax.dynamic_index_in_dim(keys_all, sequence, 0, keepdims=False)
        seq_values = lax.dynamic_index_in_dim(values_all, sequence, 0, keepdims=False)
        scores = jnp.einsum('qhd,khd->hqk', block_queries, seq_keys, precision=lax.Precision.HIGHEST) * scaling
        scores = low_back(scores)
        query_positions = start + jnp.arange(block, dtype=jnp.int32)
        allowed = key_positions[None, :] <= query_positions[:, None]
        scores = jnp.where(allowed[None], scores, -1e+30)
        top_score = lax.optimization_barrier(jnp.max(scores, axis=-1, keepdims=True))
        raised = jnp.exp(scores - top_score)
        attn_probs = raised / lax.optimization_barrier(jnp.sum(raised, axis=-1, keepdims=True))
        return jnp.einsum('hqk,khd->qhd', low(attn_probs), seq_values, precision=lax.Precision.HIGHEST)
    items = jnp.arange(SEQS * count, dtype=jnp.int32)
    blocks = lax.map(jax.checkpoint(one_block), items)
    return blocks.reshape(SEQS, SEQ_LEN, HEADS, HEAD_DIM)

def layer(residual, weights, positions):
    gain_attn, shift_attn, gain_mlp, shift_mlp, w_qkv, b_qv, w_out, b_out, w_up, b_up, w_down, b_down = weights
    seq_count, length, model_width = residual.shape
    normed_attn = low(normalize(residual, gain_attn, shift_attn))
    normed_mlp = low(normalize(residual, gain_mlp, shift_mlp))
    qkv_bias = jnp.concatenate([b_qv[:model_width], jnp.zeros((model_width,), jnp.float32), b_qv[model_width:]])
    projected = low_back(high_dot(normed_attn, w_qkv) + qkv_bias)
    split_heads = projected.reshape(seq_count, length, 3, HEADS, HEAD_DIM)
    queries = low(rotate(split_heads[:, :, 0], positions))
    keys_all = low(rotate(split_heads[:, :, 1], positions))
    values_all = low(split_heads[:, :, 2])
    context = attend(queries, keys_all, values_all).reshape(seq_count, length, model_width)
    context = low(low_back(context))
    branch_attn = low_back(high_dot(context, w_out) + b_out)
    hidden = low_back(high_dot(normed_mlp, w_up) + b_up)
    active = low(jax.nn.gelu(hidden, approximate=False))
    branch_mlp = low_back(high_dot(active, w_down) + b_down)
    return residual + branch_attn + branch_mlp

def to_order(tokens):
    early = tokens[:, 0]
    late = tokens[:, 1].reshape(SEQS, N_CTX, BLK, D)[:, ::-1].reshape(SEQS, HALF, D)
    return jnp.concatenate([early, late], axis=1)

def from_order(tokens):
    early = tokens[:, :HALF]
    late = tokens[:, HALF:].reshape(SEQS, N_CTX, BLK, D)[:, ::-1].reshape(SEQS, HALF, D)
    return jnp.stack([early, late], axis=1)

def reference(tokens_in, cotangent, ln_gain_attn, ln_shift_attn, ln_gain_mlp, ln_shift_mlp, w_qkv, b_qv, w_out, b_out, w_up, b_up, w_down, b_down):
    params = (ln_gain_attn, ln_shift_attn, ln_gain_mlp, ln_shift_mlp, w_qkv, b_qv, w_out, b_out, w_up, b_up, w_down, b_down)
    weights = tuple((param.astype(jnp.float32) for param in params))
    start = to_order(tokens_in.astype(jnp.float32))
    positions = jnp.arange(SEQ_LEN, dtype=jnp.int32)

    def forward(residual, weight_set):
        for layer_index in range(LAYERS):
            residual = layer(residual, tuple((param[layer_index] for param in weight_set)), positions)
        return residual
    result, pullback = jax.vjp(forward, start, weights)
    grad_start, grad_weights = pullback(to_order(cotangent.astype(jnp.float32)))
    return (from_order(result).astype(jnp.bfloat16), from_order(grad_start), grad_weights[0], grad_weights[1], grad_weights[2], grad_weights[3], grad_weights[4], grad_weights[5], grad_weights[6], grad_weights[7], grad_weights[8], grad_weights[9], grad_weights[10], grad_weights[11])
```

```python
import jax
import jax.numpy as jnp
from jax import lax
from jax.experimental import pallas as pl
from jax.experimental.pallas import tpu as pltpu
from jax.sharding import PartitionSpec as P

HEADS = 12
HEAD_DIM = 64
ROT = 16
LAYERS = 2
BLK = 32
EPS = 1e-05

F32 = jnp.float32
BF16 = jnp.bfloat16
NT = (((1,), (1,)), ((), ()))
NN = (((1,), (0,)), ((), ()))
TILE = 512


def dot(left, right, dims=NN):
    return lax.dot_general(left, right, dims, preferred_element_type=F32)


def exchange(chunks, axis):
    return lax.all_to_all(chunks, axis, 0, 0, tiled=True)


def spread(value, axis):
    count = lax.axis_size(axis)
    return exchange(jnp.broadcast_to(value[None], (count,) + value.shape), axis)


def tile_list(size):
    tiles = []
    for start in range(0, size, TILE):
        keys = [(0, k, k == start) for k in range(0, start + TILE, TILE)]
        tiles.append((0, start, keys))
    for start in range(0, size, TILE):
        keys = [(0, k, False) for k in range(0, size, TILE)]
        keys += [(1, k, k == start) for k in range(start, size, TILE)]
        tiles.append((1, start, keys))
    return tiles


def tile_mask(half):
    row = lax.broadcasted_iota(jnp.int32, (TILE, TILE), 0)
    col = lax.broadcasted_iota(jnp.int32, (TILE, TILE), 1)
    if half:
        shift = BLK.bit_length() - 1
        row_pos = (row & (BLK - 1)) - ((row >> shift) << shift)
        col_pos = (col & (BLK - 1)) - ((col >> shift) << shift)
        return row_pos <= col_pos
    return row <= col


def forward_kernel(in_ref, out_ref, full_ref, lse_ref, q_scr, k_scr, vt_scr):
    count = in_ref.shape[0]
    size = count * BLK
    for half in range(2):
        both = in_ref[:, half * BLK : (half + 1) * BLK, :].reshape(size, 128)
        q_scr[half] = both[:, :64] * jnp.asarray(HEAD_DIM ** -0.5, BF16)
        k_scr[half] = both[:, 64:]
    values = in_ref[:, 2 * BLK : 3 * BLK, :].reshape(size, 128)
    vt_scr[...] = values.astype(F32).T.astype(BF16)
    for half, start, keys in tile_list(size):
        query = q_scr[half, start : start + TILE, :]
        top = jnp.full((1, TILE), -1e30, F32)
        total = jnp.zeros((1, TILE), F32)
        acc = jnp.zeros((64, TILE), F32)
        for key_half, key_start, masked in keys:
            key = k_scr[key_half, key_start : key_start + TILE, :]
            scores = dot(key, query, NT)
            if masked:
                scores = jnp.where(tile_mask(half), scores, -1e30)
            new_top = jnp.maximum(top, jnp.max(scores, axis=0, keepdims=True))
            raised = jnp.exp(scores - new_top)
            keep = jnp.exp(top - new_top)
            total = total * keep + jnp.sum(raised, axis=0, keepdims=True)
            value = vt_scr[key_half * 64 : (key_half + 1) * 64, key_start : key_start + TILE]
            acc = acc * keep + dot(value, raised.astype(BF16))
            top = new_top
        full_ref[half * 64 : (half + 1) * 64, start : start + TILE] = acc / total
        lse_ref[half : half + 1, start : start + TILE] = top + jnp.log(total)
    out_ref[...] = full_ref[...].T.astype(BF16).reshape(count, BLK, 128)


def backward_kernel(in_ref, grad_ref, full_ref, lse_ref, out_ref, q_scr, k_scr, kt_scr, v_scr, do_scr, delta_scr, dq_scr, dk_scr, dv_scr):
    count = in_ref.shape[0]
    size = count * BLK
    grads = grad_ref[...].reshape(size, 128)
    grads_t = grads.astype(F32).T
    product = grads_t * full_ref[...]
    values = in_ref[:, 2 * BLK : 3 * BLK, :].reshape(size, 128)
    for half in range(2):
        both = in_ref[:, half * BLK : (half + 1) * BLK, :].reshape(size, 128)
        q_scr[half] = both[:, :64] * jnp.asarray(HEAD_DIM ** -0.5, BF16)
        k_scr[half] = both[:, 64:]
        kt_scr[half] = both.astype(F32).T[64:, :].astype(BF16)
        lanes = slice(half * 64, (half + 1) * 64)
        v_scr[half] = values[:, lanes]
        do_scr[half] = grads[:, lanes]
        delta_scr[half : half + 1, :] = jnp.sum(product[lanes, :], axis=0, keepdims=True)
    dk_scr[...] = jnp.zeros_like(dk_scr)
    dv_scr[...] = jnp.zeros_like(dv_scr)
    for half, start, keys in tile_list(size):
        rows = slice(start, start + TILE)
        query = q_scr[half, rows, :]
        grad = do_scr[half, rows, :]
        lse = lse_ref[half : half + 1, rows]
        delta = delta_scr[half : half + 1, rows]
        acc = jnp.zeros((64, TILE), F32)
        for key_half, key_start, masked in keys:
            key_rows = slice(key_start, key_start + TILE)
            scores = dot(k_scr[key_half, key_rows, :], query, NT)
            if masked:
                scores = jnp.where(tile_mask(half), scores, -1e30)
            probs = jnp.exp(scores - lse)
            grad_probs = dot(v_scr[key_half, key_rows, :], grad, NT)
            grad_scores = (probs * (grad_probs - delta)).astype(BF16)
            dv_scr[key_half, key_rows, :] += dot(probs.astype(BF16), grad)
            dk_scr[key_half, key_rows, :] += dot(grad_scores, query)
            acc += dot(kt_scr[key_half, :, key_rows], grad_scores)
        dq_scr[half * 64 : (half + 1) * 64, rows] = acc * (HEAD_DIM ** -0.5)
    queries = dq_scr[...].T
    for half in range(2):
        both = jnp.concatenate([queries[:, half * 64 : (half + 1) * 64], dk_scr[half]], axis=1)
        out_ref[:, half * BLK : (half + 1) * BLK, :] = both.astype(BF16).reshape(count, BLK, 128)
    both = jnp.concatenate([dv_scr[0], dv_scr[1]], axis=1)
    out_ref[:, 2 * BLK : 3 * BLK, :] = both.astype(BF16).reshape(count, BLK, 128)


def attend(packed):
    count = packed.shape[0]
    size = count * BLK
    return pl.pallas_call(
        forward_kernel,
        out_shape=(
            jax.ShapeDtypeStruct((count, BLK, 128), BF16),
            jax.ShapeDtypeStruct((128, size), F32),
            jax.ShapeDtypeStruct((8, size), F32),
        ),
        in_specs=[pl.BlockSpec(memory_space=pltpu.VMEM)],
        out_specs=[pl.BlockSpec(memory_space=pltpu.VMEM)] * 3,
        scratch_shapes=[
            pltpu.VMEM((2, size, 64), BF16),
            pltpu.VMEM((2, size, 64), BF16),
            pltpu.VMEM((128, size), BF16),
        ],
        compiler_params=pltpu.CompilerParams(vmem_limit_bytes=48 << 20),
        cost_estimate=pl.CostEstimate(flops=20_000_000_000, bytes_accessed=20_000_000, transcendentals=2_600_000),
        name="attend",
    )(packed)


def attend_back(packed, grads, full, lse):
    count = packed.shape[0]
    size = count * BLK
    return pl.pallas_call(
        backward_kernel,
        out_shape=jax.ShapeDtypeStruct((count, 3 * BLK, 128), BF16),
        in_specs=[pl.BlockSpec(memory_space=pltpu.VMEM)] * 4,
        out_specs=pl.BlockSpec(memory_space=pltpu.VMEM),
        scratch_shapes=[
            pltpu.VMEM((2, size, 64), BF16),
            pltpu.VMEM((2, size, 64), BF16),
            pltpu.VMEM((2, 64, size), BF16),
            pltpu.VMEM((2, size, 64), BF16),
            pltpu.VMEM((2, size, 64), BF16),
            pltpu.VMEM((8, size), F32),
            pltpu.VMEM((128, size), F32),
            pltpu.VMEM((2, size, 64), F32),
            pltpu.VMEM((2, size, 64), F32),
        ],
        compiler_params=pltpu.CompilerParams(vmem_limit_bytes=48 << 20),
        cost_estimate=pl.CostEstimate(flops=40_000_000_000, bytes_accessed=40_000_000, transcendentals=2_600_000),
        name="attend_back",
    )(packed, grads, full, lse)


def pack_rows(value, seqs):
    split = value.reshape(seqs, 2, BLK, HEADS, HEAD_DIM).transpose(0, 3, 2, 1, 4)
    return split.reshape(seqs * HEADS, BLK, 2 * HEAD_DIM)


def unpack_rows(tiles, seqs):
    split = tiles.reshape(seqs, HEADS, BLK, 2, HEAD_DIM).transpose(0, 3, 2, 1, 4)
    return split.reshape(seqs * 2 * BLK, HEADS * HEAD_DIM)


def pad_pairs(tiles):
    missing = lax.axis_size("ctx") - tiles.shape[0]
    return jnp.pad(tiles, ((0, missing), (0, 0), (0, 0)))


def pack_mixed(query, key, value, seqs):
    pair = jnp.concatenate(
        [query.reshape(seqs, 2 * BLK, HEADS, HEAD_DIM), key.reshape(seqs, 2 * BLK, HEADS, HEAD_DIM)], axis=-1
    )
    pair = pair.transpose(0, 2, 1, 3).reshape(seqs * HEADS, 2 * BLK, 2 * HEAD_DIM)
    return pad_pairs(jnp.concatenate([pair, pack_rows(value, seqs)], axis=1))


def unpack_mixed(tiles, seqs):
    pair = tiles[: seqs * HEADS, : 2 * BLK].reshape(seqs, HEADS, 2 * BLK, 2, HEAD_DIM)
    pair = pair.transpose(3, 0, 2, 1, 4).reshape(2, seqs * 2 * BLK, HEADS * HEAD_DIM)
    return pair[0], pair[1], unpack_rows(tiles[: seqs * HEADS, 2 * BLK :], seqs)


def rotary_tables(seqs):
    device = lax.axis_index("ctx")
    devices = lax.axis_size("ctx")
    offsets = jnp.arange(BLK, dtype=jnp.int32)
    early = device * BLK + offsets
    late = 2 * BLK * devices - (device + 1) * BLK + offsets
    positions = jnp.tile(jnp.concatenate([early, late]), seqs).astype(F32)
    half = ROT // 2
    frequency = 10000.0 ** (-jnp.arange(half, dtype=F32) * 2.0 / ROT)
    angles = positions[:, None] * frequency[None, :]
    cosine, sine = lax.optimization_barrier((jnp.cos(angles), jnp.sin(angles)))
    rows = positions.shape[0]
    zero = jnp.zeros((rows, half), F32)
    rest = HEAD_DIM - ROT

    def whole(first, second, fill):
        return jnp.tile(jnp.concatenate([first, second, jnp.full((rows, rest), fill, F32)], axis=1), (1, HEADS))

    tables = (whole(cosine, cosine, 1.0), whole(zero, sine, 0.0), whole(sine, zero, 0.0))
    return lax.optimization_barrier(tables)


def turn(value, tables, sign):
    cosine, up, down = tables
    half = ROT // 2
    return value * cosine + sign * (jnp.roll(value, half, 1) * up - jnp.roll(value, -half, 1) * down)


def standardize(values):
    centred = values - jnp.mean(values, axis=-1, keepdims=True)
    scale = lax.rsqrt(jnp.mean(centred * centred, axis=-1, keepdims=True) + EPS)
    return centred * scale, scale


def cdf(value):
    return 0.5 * (1.0 + lax.erf(value * (0.5 ** 0.5)))


def layer_forward(x, w, tables, seqs):
    xhat, scale = standardize(x)
    xhat_low = xhat.astype(BF16)
    xhat_all = spread(xhat_low, "wt").reshape(-1, x.shape[1])
    n_attn = (xhat * w["g_attn"] + w["s_attn"]).astype(BF16)
    mixed = dot(n_attn, w["qkv"])
    width = x.shape[1]
    query = turn(mixed[:, :width] + w["b_q"], tables, 1.0).astype(BF16)
    key = turn(mixed[:, width : 2 * width], tables, 1.0).astype(BF16)
    value = (mixed[:, 2 * width :] + w["b_v"]).astype(BF16)
    packed = exchange(pack_mixed(query, key, value, seqs), "ctx")
    out, full, lse = attend(packed)
    context = unpack_rows(exchange(out, "ctx")[: seqs * HEADS], seqs)
    n_mlp_all = (xhat_all.astype(F32) * w["g_mlp"] + w["s_mlp"]).astype(BF16)
    hidden = dot(n_mlp_all, w["up"]) + w["b_up"]
    active = (hidden * cdf(hidden)).astype(BF16)
    partial = dot(active, w["down"]).astype(BF16)
    mlp = exchange(partial.reshape(-1, *x.shape), "wt").astype(F32).sum(0)
    branch = dot(context, w["out"]) + w["b_out"]
    group = lax.axis_size("wt")
    context_all = exchange(context.reshape(x.shape[0], group, -1).transpose(1, 0, 2), "wt")
    stored = (xhat, scale, xhat_all, n_mlp_all, packed, full, lse, context_all, hidden, active)
    return x + branch + (mlp + w["b_down"]), stored


def layer_backward(g, w, stored, tables, seqs):
    xhat, scale, xhat_all, n_mlp_all, packed, full, lse, context_all, hidden, active = stored
    rows, width = g.shape
    group = lax.axis_size("wt")
    g_low = g.astype(BF16)
    g_all = spread(g_low, "wt").reshape(-1, width)
    grad_context = dot(g_low, w["out"], NT).astype(BF16)
    grads = exchange(pad_pairs(pack_rows(grad_context, seqs)), "ctx")
    grad_active = dot(g_all, w["down"], NT)
    density = jnp.exp(-0.5 * hidden * hidden) * 0.3989422804014327
    grad_hidden = (grad_active * (cdf(hidden) + hidden * density)).astype(BF16)
    partial = dot(grad_hidden, w["up"], NT).astype(BF16)
    grad_n_mlp = exchange(partial.reshape(-1, rows, width), "wt").astype(F32).sum(0)
    tn = (((0,), (0,)), ((), ()))
    grad_down = dot(active, g_all, tn).astype(BF16)
    grad_out = dot(context_all.transpose(2, 0, 1).reshape(width // group, -1), g_all).astype(BF16)
    grad_up = dot(n_mlp_all, grad_hidden, tn).astype(BF16)
    grad_b_up = jnp.sum(grad_hidden.astype(F32), axis=0)
    grad_up = exchange(grad_up.reshape(group, width // group, -1), "wt").reshape(width, -1)
    sums = jnp.concatenate([grad_down, grad_up, grad_out], axis=0)
    pieces = exchange(sums.reshape(lax.axis_size("ctx"), -1, width), "ctx")
    wide = spread(pieces.astype(F32).sum(0).astype(BF16), "ctx").reshape(-1, width)
    back = exchange(attend_back(packed, grads, full, lse), "ctx")
    grad_q, grad_k, grad_v = unpack_mixed(back, seqs)
    grad_q = turn(grad_q.astype(F32), tables, -1.0).astype(BF16)
    grad_k = turn(grad_k.astype(F32), tables, -1.0).astype(BF16)
    grad_mixed = jnp.concatenate([grad_q, grad_k, grad_v], axis=1)
    grad_n_attn = dot(grad_mixed, w["qkv"], NT)
    mixed_all = exchange(grad_mixed.reshape(rows, group, -1).transpose(1, 0, 2), "wt").reshape(group * rows, -1)
    n_attn_all = (xhat_all.astype(F32) * w["g_attn"] + w["s_attn"]).astype(BF16)
    grad_qkv = dot(n_attn_all, mixed_all, tn).astype(BF16).reshape(group, width // group, -1)
    pull = grad_n_attn * w["g_attn"] + grad_n_mlp * w["g_mlp"]
    inner = pull - jnp.mean(pull, axis=-1, keepdims=True) - xhat * jnp.mean(pull * xhat, axis=-1, keepdims=True)
    small = jnp.stack(
        [
            jnp.sum(grad_n_attn * xhat, axis=0),
            jnp.sum(grad_n_attn, axis=0),
            jnp.sum(grad_n_mlp * xhat, axis=0),
            jnp.sum(grad_n_mlp, axis=0),
            jnp.sum(g_low.astype(F32), axis=0),
        ]
    )
    bias = jnp.concatenate([jnp.sum(grad_q.astype(F32), axis=0), jnp.sum(grad_v.astype(F32), axis=0)])
    small = small.reshape(5, group, -1).transpose(1, 0, 2).reshape(group, -1)
    small = jnp.concatenate([small, bias.reshape(group, -1)], axis=1)
    return g + scale * inner, wide, grad_qkv, small, grad_b_up


def gather_small(stacked):
    names = ("g_attn", "s_attn", "g_mlp", "s_mlp", "b_qv", "b_out", "b_down")
    flat = jnp.concatenate([stacked[name] for name in names], axis=1)
    every = lax.all_gather(flat, "wt", axis=0).astype(F32)
    found, at = {}, 0
    for name in names:
        size = stacked[name].shape[1]
        found[name] = every[:, :, at : at + size].transpose(1, 0, 2).reshape(LAYERS, -1)
        at += size
    return found


def local(tokens_in, cotangent, ln_gain_attn, ln_shift_attn, ln_gain_mlp, ln_shift_mlp, w_qkv, b_qv, w_out, b_out, w_up, b_up, w_down, b_down):
    seqs = tokens_in.shape[0]
    width = tokens_in.shape[3]
    rows = seqs * 2 * BLK
    group = lax.axis_size("wt")
    devices = lax.axis_size("ctx")
    tables = rotary_tables(seqs)
    small = gather_small(
        {"g_attn": ln_gain_attn, "s_attn": ln_shift_attn, "g_mlp": ln_gain_mlp, "s_mlp": ln_shift_mlp, "b_qv": b_qv, "b_out": b_out, "b_down": b_down}
    )
    layers = []
    for layer in range(LAYERS):
        up = w_up[layer].reshape(width // group, group, -1).transpose(1, 0, 2)
        w = {name: small[name][layer][None] for name in small}
        w["b_q"] = w["b_qv"][:, :width]
        w["b_v"] = w["b_qv"][:, width:]
        w["qkv"] = lax.all_gather(w_qkv[layer], "wt", axis=0, tiled=True)
        w["out"] = lax.all_gather(w_out[layer], "wt", axis=0, tiled=True)
        w["up"] = exchange(up, "wt").reshape(width, -1)
        w["down"] = w_down[layer]
        w["b_up"] = b_up[layer].astype(F32)[None]
        layers.append(w)
    x = tokens_in.reshape(rows, width).astype(F32)
    kept = []
    for w in layers:
        x, stored = layer_forward(x, w, tables, seqs)
        kept.append(stored)
    out_tokens = x.astype(BF16).reshape(tokens_in.shape)
    g = cotangent.reshape(rows, width).astype(F32)
    wides, qkvs, smalls, ups = ([None] * LAYERS for _ in range(4))
    for layer in reversed(range(LAYERS)):
        g, wides[layer], qkvs[layer], smalls[layer], ups[layer] = layer_backward(g, layers[layer], kept[layer], tables, seqs)
    columns = qkvs[0].shape[2]
    depth = width // group
    piece = width // devices

    def to_rows(value):
        size = value.shape[-1]
        lines = -(-size // columns)
        lines = -(-lines // 8) * 8
        padded = jnp.pad(value, ((0, 0), (0, lines * columns - size)))
        return padded.reshape(value.shape[0], lines, columns)

    totals = [None] * LAYERS
    for layer in reversed(range(1, LAYERS)):
        moved = exchange(qkvs[layer], "wt")
        part = exchange(moved.reshape(devices, piece, columns), "ctx").astype(F32).sum(0).astype(BF16)
        totals[layer] = spread(part, "ctx").reshape(group, depth, columns)
    tiny = to_rows(jnp.concatenate(smalls, axis=1).astype(BF16))
    moved = exchange(jnp.concatenate([qkvs[0], tiny], axis=1), "wt")
    small_sum = moved[:, depth:].astype(F32).sum(0).reshape(1, -1)[:, : sum(s.shape[1] for s in smalls)]
    tail = to_rows(jnp.concatenate([small_sum, *(u[None] for u in ups)], axis=1).astype(BF16))
    sent = jnp.concatenate(
        [moved[:, :depth].reshape(devices, piece, columns), jnp.broadcast_to(tail, (devices,) + tail.shape[1:])], axis=1
    )
    landed = exchange(sent, "ctx").astype(F32).sum(0)
    totals[0] = spread(landed[:piece].astype(BF16), "ctx").reshape(group, depth, columns)
    flat = landed[piece:].reshape(-1)
    tiny_size = smalls[0].shape[1]
    per_layer = [flat[layer * tiny_size : (layer + 1) * tiny_size] for layer in range(LAYERS)]
    at = LAYERS * tiny_size
    unit = ups[0].shape[0]
    grad_b_up = flat[at : at + LAYERS * unit].reshape(LAYERS, unit)

    def vector(index):
        return jnp.stack([v[index * depth : (index + 1) * depth] for v in per_layer])

    grad_bias = vector(4)
    grad_b_qv = jnp.stack([v[5 * depth :] for v in per_layer])
    grad_qkv = jnp.stack([t.astype(F32).transpose(1, 0, 2).reshape(depth, -1) for t in totals])
    grad_down = jnp.stack([v[:unit].astype(F32) for v in wides])
    grad_up = jnp.stack(
        [v[unit : unit + width].astype(F32).reshape(group, depth, unit).transpose(1, 0, 2).reshape(depth, -1) for v in wides]
    )
    grad_out = jnp.stack([v[unit + width :].astype(F32) for v in wides])
    return (
        out_tokens,
        g.reshape(tokens_in.shape),
        vector(0),
        vector(1),
        vector(2),
        vector(3),
        grad_qkv,
        grad_b_qv,
        grad_out,
        grad_bias,
        grad_up,
        grad_b_up,
        grad_down,
        grad_bias,
    )


def solution(mesh):
    tokens = P("wt", None, "ctx", None)
    vec, mat = P(None, "wt"), P(None, "wt", None)
    params = (vec, vec, vec, vec, mat, vec, mat, vec, mat, vec, mat, vec)
    return jax.shard_map(
        local,
        mesh=mesh,
        in_specs=(tokens, tokens) + params,
        out_specs=(tokens, tokens) + params,
        check_vma=False,
    )
```

```python
import jax
import jax.numpy as jnp
from jax import lax
from jax.experimental import pallas as pl
from jax.experimental.pallas import tpu as pltpu
from jax.sharding import PartitionSpec as P

HEADS = 12
HEAD_DIM = 64
ROT = 16
LAYERS = 2
BLK = 32
EPS = 1e-05

F32 = jnp.float32
BF16 = jnp.bfloat16
NT = (((1,), (1,)), ((), ()))
NN = (((1,), (0,)), ((), ()))
TILE = 512


def dot(left, right, dims=NN):
    return lax.dot_general(left, right, dims, preferred_element_type=F32)


def exchange(chunks, axis):
    return lax.all_to_all(chunks, axis, 0, 0, tiled=True)


def pass_on(value, shift):
    count = lax.axis_size("wt")
    return lax.ppermute(value, "wt", [(i, (i + shift) % count) for i in range(count)])


def shifts():
    return (1, 3, 2)


def group_spread(value):
    landed = {0: value}
    for shift in shifts():
        landed[shift] = pass_on(value, shift)
    return [landed[shift] for shift in range(4)]


def group_sum(blocks):
    total = blocks[0]
    for shift in shifts():
        total = total + pass_on(blocks[shift].astype(BF16), (4 - shift) % 4).astype(F32)
    return total


def group_trade(chunks):
    here = lax.axis_index("wt")

    def chunk(shift):
        return lax.dynamic_index_in_dim(chunks, (here + shift) % 4, 0, keepdims=False)

    landed = {0: chunk(0)}
    for shift in shifts():
        landed[shift] = pass_on(chunk(shift), shift)
    return [landed[shift] for shift in range(4)]


def place(blocks, axis):
    here = lax.axis_index("wt")
    shape = list(blocks[0].shape)
    size = shape[axis]
    shape[axis] = 4 * size
    whole = jnp.zeros(shape, blocks[0].dtype)
    for shift in range(4):
        whole = lax.dynamic_update_slice_in_dim(whole, blocks[shift], ((here - shift) % 4) * size, axis)
    return whole


def swap(value):
    return lax.ppermute(value, "ctx", [(i, i ^ 1) for i in range(lax.axis_size("ctx"))])


def gather_half(shard):
    core = lax.axis_index("ctx") % 2
    half = shard.shape[0] // 2
    mine = lax.dynamic_slice_in_dim(shard, core * half, half, 0)
    return place([b[None] for b in group_spread(mine)], 0)


def gather_rest(here):
    core = lax.axis_index("ctx") % 2
    other = swap(here)
    first = jnp.where(core == 0, here, other)
    second = jnp.where(core == 0, other, here)
    return jnp.stack([first, second], axis=1).reshape(-1, here.shape[2])


def after(values, first):
    return lax.optimization_barrier((values, first))[0]


def spread(value, axis):
    count = lax.axis_size(axis)
    return exchange(jnp.broadcast_to(value[None], (count,) + value.shape), axis)


def tile_list(size):
    tiles = []
    for start in range(0, size, TILE):
        keys = [(0, k, k == start) for k in range(0, start + TILE, TILE)]
        tiles.append((0, start, keys))
    for start in range(0, size, TILE):
        keys = [(0, k, False) for k in range(0, size, TILE)]
        keys += [(1, k, k == start) for k in range(start, size, TILE)]
        tiles.append((1, start, keys))
    return tiles


def tile_mask(half):
    row = lax.broadcasted_iota(jnp.int32, (TILE, TILE), 0)
    col = lax.broadcasted_iota(jnp.int32, (TILE, TILE), 1)
    if half:
        shift = BLK.bit_length() - 1
        row_pos = (row & (BLK - 1)) - ((row >> shift) << shift)
        col_pos = (col & (BLK - 1)) - ((col >> shift) << shift)
        return row_pos <= col_pos
    return row <= col


def forward_kernel(in_ref, out_ref, full_ref, lse_ref, q_scr, k_scr, vt_scr):
    count = in_ref.shape[0]
    size = count * BLK
    for half in range(2):
        both = in_ref[:, half * BLK : (half + 1) * BLK, :].reshape(size, 128)
        q_scr[half] = both[:, :64] * jnp.asarray(HEAD_DIM ** -0.5, BF16)
        k_scr[half] = both[:, 64:]
    values = in_ref[:, 2 * BLK : 3 * BLK, :].reshape(size, 128)
    vt_scr[...] = values.astype(F32).T.astype(BF16)
    for half, start, keys in tile_list(size):
        query = q_scr[half, start : start + TILE, :]
        top = jnp.full((1, TILE), -1e30, F32)
        total = jnp.zeros((1, TILE), F32)
        acc = jnp.zeros((64, TILE), F32)
        for key_half, key_start, masked in keys:
            key = k_scr[key_half, key_start : key_start + TILE, :]
            scores = dot(key, query, NT)
            if masked:
                scores = jnp.where(tile_mask(half), scores, -1e30)
            new_top = jnp.maximum(top, jnp.max(scores, axis=0, keepdims=True))
            raised = jnp.exp(scores - new_top)
            keep = jnp.exp(top - new_top)
            total = total * keep + jnp.sum(raised, axis=0, keepdims=True)
            value = vt_scr[key_half * 64 : (key_half + 1) * 64, key_start : key_start + TILE]
            acc = acc * keep + dot(value, raised.astype(BF16))
            top = new_top
        full_ref[half * 64 : (half + 1) * 64, start : start + TILE] = acc / total
        lse_ref[half : half + 1, start : start + TILE] = top + jnp.log(total)
    out_ref[...] = full_ref[...].T.astype(BF16).reshape(count, BLK, 128)


def backward_kernel(in_ref, grad_ref, full_ref, lse_ref, out_ref, q_scr, k_scr, kt_scr, v_scr, do_scr, delta_scr, dq_scr, dk_scr, dv_scr):
    count = in_ref.shape[0]
    size = count * BLK
    grads = grad_ref[...].reshape(size, 128)
    grads_t = grads.astype(F32).T
    product = grads_t * full_ref[...]
    values = in_ref[:, 2 * BLK : 3 * BLK, :].reshape(size, 128)
    for half in range(2):
        both = in_ref[:, half * BLK : (half + 1) * BLK, :].reshape(size, 128)
        q_scr[half] = both[:, :64] * jnp.asarray(HEAD_DIM ** -0.5, BF16)
        k_scr[half] = both[:, 64:]
        kt_scr[half] = both.astype(F32).T[64:, :].astype(BF16)
        lanes = slice(half * 64, (half + 1) * 64)
        v_scr[half] = values[:, lanes]
        do_scr[half] = grads[:, lanes]
        delta_scr[half : half + 1, :] = jnp.sum(product[lanes, :], axis=0, keepdims=True)
    dk_scr[...] = jnp.zeros_like(dk_scr)
    dv_scr[...] = jnp.zeros_like(dv_scr)
    for half, start, keys in tile_list(size):
        rows = slice(start, start + TILE)
        query = q_scr[half, rows, :]
        grad = do_scr[half, rows, :]
        lse = lse_ref[half : half + 1, rows]
        delta = delta_scr[half : half + 1, rows]
        acc = jnp.zeros((64, TILE), F32)
        for key_half, key_start, masked in keys:
            key_rows = slice(key_start, key_start + TILE)
            scores = dot(k_scr[key_half, key_rows, :], query, NT)
            if masked:
                scores = jnp.where(tile_mask(half), scores, -1e30)
            probs = jnp.exp(scores - lse)
            grad_probs = dot(v_scr[key_half, key_rows, :], grad, NT)
            grad_scores = (probs * (grad_probs - delta)).astype(BF16)
            dv_scr[key_half, key_rows, :] += dot(probs.astype(BF16), grad)
            dk_scr[key_half, key_rows, :] += dot(grad_scores, query)
            acc += dot(kt_scr[key_half, :, key_rows], grad_scores)
        dq_scr[half * 64 : (half + 1) * 64, rows] = acc * (HEAD_DIM ** -0.5)
    queries = dq_scr[...].T
    for half in range(2):
        both = jnp.concatenate([queries[:, half * 64 : (half + 1) * 64], dk_scr[half]], axis=1)
        out_ref[:, half * BLK : (half + 1) * BLK, :] = both.astype(BF16).reshape(count, BLK, 128)
    both = jnp.concatenate([dv_scr[0], dv_scr[1]], axis=1)
    out_ref[:, 2 * BLK : 3 * BLK, :] = both.astype(BF16).reshape(count, BLK, 128)


def attend(packed):
    count = packed.shape[0]
    size = count * BLK
    return pl.pallas_call(
        forward_kernel,
        out_shape=(
            jax.ShapeDtypeStruct((count, BLK, 128), BF16),
            jax.ShapeDtypeStruct((128, size), F32),
            jax.ShapeDtypeStruct((8, size), F32),
        ),
        in_specs=[pl.BlockSpec(memory_space=pltpu.VMEM)],
        out_specs=[pl.BlockSpec(memory_space=pltpu.VMEM)] * 3,
        scratch_shapes=[
            pltpu.VMEM((2, size, 64), BF16),
            pltpu.VMEM((2, size, 64), BF16),
            pltpu.VMEM((128, size), BF16),
        ],
        compiler_params=pltpu.CompilerParams(vmem_limit_bytes=48 << 20),
        cost_estimate=pl.CostEstimate(flops=20_000_000_000, bytes_accessed=20_000_000, transcendentals=2_600_000),
        name="attend",
    )(packed)


def attend_back(packed, grads, full, lse):
    count = packed.shape[0]
    size = count * BLK
    return pl.pallas_call(
        backward_kernel,
        out_shape=jax.ShapeDtypeStruct((count, 3 * BLK, 128), BF16),
        in_specs=[pl.BlockSpec(memory_space=pltpu.VMEM)] * 4,
        out_specs=pl.BlockSpec(memory_space=pltpu.VMEM),
        scratch_shapes=[
            pltpu.VMEM((2, size, 64), BF16),
            pltpu.VMEM((2, size, 64), BF16),
            pltpu.VMEM((2, 64, size), BF16),
            pltpu.VMEM((2, size, 64), BF16),
            pltpu.VMEM((2, size, 64), BF16),
            pltpu.VMEM((8, size), F32),
            pltpu.VMEM((128, size), F32),
            pltpu.VMEM((2, size, 64), F32),
            pltpu.VMEM((2, size, 64), F32),
        ],
        compiler_params=pltpu.CompilerParams(vmem_limit_bytes=48 << 20),
        cost_estimate=pl.CostEstimate(flops=40_000_000_000, bytes_accessed=40_000_000, transcendentals=2_600_000),
        name="attend_back",
    )(packed, grads, full, lse)


def kernel_turn(value, tables, sign):
    cosine, up, down = tables
    half = ROT // 2
    back = value.shape[1] - half
    turned = pltpu.roll(value, half, 1) * up - pltpu.roll(value, back, 1) * down
    return value * cosine + sign * turned


def head(value, rows, index):
    return value[rows, index * HEAD_DIM : (index + 1) * HEAD_DIM]


def mix_kernel(x_ref, gain_ref, shift_ref, w_ref, bq_ref, bv_ref, cos_ref, up_ref, down_ref, xhat_ref, low_ref, scale_ref, out_ref):
    x = x_ref[...]
    rows, width = x.shape
    centred = x - jnp.mean(x, axis=-1, keepdims=True)
    scale = lax.rsqrt(jnp.mean(centred * centred, axis=-1, keepdims=True) + EPS)
    xhat = centred * scale
    xhat_ref[...] = xhat
    low_ref[...] = xhat.astype(BF16)
    scale_ref[...] = jnp.broadcast_to(scale, scale_ref.shape)
    normed = (xhat * gain_ref[...] + shift_ref[...]).astype(BF16)
    tables = (cos_ref[...], up_ref[...], down_ref[...])
    query = kernel_turn(dot(normed, w_ref[:, :width]) + bq_ref[...], tables, 1.0)
    key = kernel_turn(dot(normed, w_ref[:, width : 2 * width]), tables, 1.0)
    value = dot(normed, w_ref[:, 2 * width :]) + bv_ref[...]
    seqs = rows // (2 * BLK)
    for s in range(seqs):
        at = s * 2 * BLK
        whole, early, late = slice(at, at + 2 * BLK), slice(at, at + BLK), slice(at + BLK, at + 2 * BLK)
        for h in range(HEADS):
            pair = jnp.concatenate([head(query, whole, h), head(key, whole, h)], axis=1)
            out_ref[s * HEADS + h, : 2 * BLK, :] = pair.astype(BF16)
            pair = jnp.concatenate([head(value, early, h), head(value, late, h)], axis=1)
            out_ref[s * HEADS + h, 2 * BLK :, :] = pair.astype(BF16)
    spare = out_ref.shape[0] - seqs * HEADS
    out_ref[seqs * HEADS :, :, :] = jnp.zeros((spare,) + out_ref.shape[1:], BF16)


def on_chip(kernel, out_shape, name, flops, *operands, scratch=()):
    many = isinstance(out_shape, tuple)
    spec = pl.BlockSpec(memory_space=pltpu.VMEM)
    return pl.pallas_call(
        kernel,
        out_shape=out_shape,
        in_specs=[spec] * len(operands),
        out_specs=[spec] * len(out_shape) if many else spec,
        scratch_shapes=list(scratch),
        compiler_params=pltpu.CompilerParams(vmem_limit_bytes=48 << 20),
        cost_estimate=pl.CostEstimate(flops=flops, bytes_accessed=8_000_000, transcendentals=0),
        name=name,
    )(*operands)


def shaped(shape, dtype):
    return jax.ShapeDtypeStruct(shape, dtype)


def mix(x, w, tables):
    rows, width = x.shape
    count = lax.axis_size("ctx")
    shapes = (
        shaped((rows, width), F32),
        shaped((rows, width), BF16),
        shaped((rows, 128), F32),
        shaped((count, 3 * BLK, 128), BF16),
    )
    return on_chip(mix_kernel, shapes, "mix", 5_000_000_000, x, w["g_attn"], w["s_attn"], w["qkv"], w["b_q"], w["b_v"], *tables)


def join_kernel(tile_ref, x_ref, mlp_ref, w_ref, bias_ref, split_ref, out_ref, context):
    rows, width = context.shape
    for s in range(rows // (2 * BLK)):
        for half in range(2):
            at = (2 * s + half) * BLK
            lanes = slice(half * HEAD_DIM, (half + 1) * HEAD_DIM)
            row = [tile_ref[s * HEADS + h, :, lanes] for h in range(HEADS)]
            context[at : at + BLK, :] = jnp.concatenate(row, axis=1)
    size = width // 4
    for block in range(4):
        split_ref[block] = context[:, block * size : (block + 1) * size]
    out_ref[...] = x_ref[...] + dot(context[...], w_ref[...]) + (mlp_ref[...] + bias_ref[...])


def join(tiles, x, mlp, w):
    rows, width = x.shape
    shapes = (shaped((4, rows, width // 4), BF16), shaped((rows, width), F32))
    scratch = [pltpu.VMEM((rows, width), BF16)]
    return on_chip(join_kernel, shapes, "join", 500_000_000, tiles, x, mlp, w["out"], w["b_out"] + w["b_down"], scratch=scratch)


def pull_kernel(g_ref, w_ref, out_ref):
    grad = dot(g_ref[...], w_ref[...], NT)
    seqs = grad.shape[0] // (2 * BLK)
    for s in range(seqs):
        at = s * 2 * BLK
        for h in range(HEADS):
            early, late = head(grad, slice(at, at + BLK), h), head(grad, slice(at + BLK, at + 2 * BLK), h)
            out_ref[s * HEADS + h] = jnp.concatenate([early, late], axis=1).astype(BF16)
    spare = out_ref.shape[0] - seqs * HEADS
    out_ref[seqs * HEADS :, :, :] = jnp.zeros((spare,) + out_ref.shape[1:], BF16)


def pull(g_low, w):
    count = lax.axis_size("ctx")
    return on_chip(pull_kernel, shaped((count, BLK, 128), BF16), "pull", 500_000_000, g_low, w["out"])


def unmix_kernel(tile_ref, cos_ref, up_ref, down_ref, mixed_ref, split_ref, sums_ref):
    rows, width = cos_ref.shape
    tables = (cos_ref[...], up_ref[...], down_ref[...])
    parts = [[], [], []]
    for s in range(rows // (2 * BLK)):
        for part in range(2):
            lanes = slice(part * HEAD_DIM, (part + 1) * HEAD_DIM)
            row = [tile_ref[s * HEADS + h, : 2 * BLK, lanes] for h in range(HEADS)]
            parts[part].append(jnp.concatenate(row, axis=1))
        for half in range(2):
            lanes = slice(half * HEAD_DIM, (half + 1) * HEAD_DIM)
            row = [tile_ref[s * HEADS + h, 2 * BLK :, lanes] for h in range(HEADS)]
            parts[2].append(jnp.concatenate(row, axis=1))
    query, key, value = (jnp.concatenate(part, axis=0) for part in parts)
    mixed_ref[:, :width] = kernel_turn(query.astype(F32), tables, -1.0).astype(BF16)
    mixed_ref[:, width : 2 * width] = kernel_turn(key.astype(F32), tables, -1.0).astype(BF16)
    mixed_ref[:, 2 * width :] = value
    size = 3 * width // 4
    for block in range(4):
        split_ref[block] = mixed_ref[:, block * size : (block + 1) * size]
    sums_ref[...] = jnp.sum(mixed_ref[...].astype(F32), axis=0, keepdims=True)


def unmix(tiles, tables):
    rows, width = tables[0].shape
    shapes = (
        shaped((rows, 3 * width), BF16),
        shaped((4, rows, 3 * width // 4), BF16),
        shaped((1, 3 * width), F32),
    )
    return on_chip(unmix_kernel, shapes, "unmix", 500_000_000, tiles, *tables)


def norm_kernel(mixed_ref, w_ref, g_ref, mlp_ref, xhat_ref, scale_ref, ga_ref, gm_ref, out_ref, low_ref, sums_ref):
    attn = dot(mixed_ref[...], w_ref[...], NT)
    mlp, xhat, g = mlp_ref[...], xhat_ref[...], g_ref[...]
    both = attn * ga_ref[...] + mlp * gm_ref[...]
    inner = both - jnp.mean(both, axis=-1, keepdims=True) - xhat * jnp.mean(both * xhat, axis=-1, keepdims=True)
    new = g + scale_ref[:, :1] * inner
    out_ref[...] = new
    low_ref[...] = new.astype(BF16)
    sums_ref[...] = jnp.zeros_like(sums_ref)
    for row, value in enumerate((attn * xhat, attn, mlp * xhat, mlp, g.astype(BF16).astype(F32))):
        sums_ref[row : row + 1, :] = jnp.sum(value, axis=0, keepdims=True)


def norm_backward(g, mixed, grad_n_mlp, xhat, scale, w):
    rows, width = g.shape
    shapes = (shaped((rows, width), F32), shaped((rows, width), BF16), shaped((8, width), F32))
    return on_chip(
        norm_kernel, shapes, "norm_back", 1_500_000_000, mixed, w["qkv"], g, grad_n_mlp, xhat, scale, w["g_attn"], w["g_mlp"]
    )


def rotary_tables(seqs):
    device = lax.axis_index("ctx")
    devices = lax.axis_size("ctx")
    offsets = jnp.arange(BLK, dtype=jnp.int32)
    early = device * BLK + offsets
    late = 2 * BLK * devices - (device + 1) * BLK + offsets
    positions = jnp.tile(jnp.concatenate([early, late]), seqs).astype(F32)
    half = ROT // 2
    frequency = 10000.0 ** (-jnp.arange(half, dtype=F32) * 2.0 / ROT)
    angles = positions[:, None] * frequency[None, :]
    cosine, sine = lax.optimization_barrier((jnp.cos(angles), jnp.sin(angles)))
    rows = positions.shape[0]
    zero = jnp.zeros((rows, half), F32)
    rest = HEAD_DIM - ROT

    def whole(first, second, fill):
        return jnp.tile(jnp.concatenate([first, second, jnp.full((rows, rest), fill, F32)], axis=1), (1, HEADS))

    tables = (whole(cosine, cosine, 1.0), whole(zero, sine, 0.0), whole(sine, zero, 0.0))
    return lax.optimization_barrier(tables)


def cdf(value):
    return 0.5 * (1.0 + lax.erf(value * (0.5 ** 0.5)))


TN = (((0,), (0,)), ((), ()))


def split_columns(value):
    return value.reshape(value.shape[0], 4, -1).transpose(1, 0, 2)


def mlp_forward(xhat_all, w):
    n_mlp_all = (xhat_all.astype(F32) * w["g_mlp"] + w["s_mlp"]).astype(BF16)
    hidden = dot(n_mlp_all, w["up"]) + w["b_up"]
    active = (hidden * cdf(hidden)).astype(BF16)
    partial = dot(active, w["down"])
    rows = partial.shape[0] // 4
    total = group_sum([partial[i * rows : (i + 1) * rows] for i in range(4)])
    return n_mlp_all, hidden, active, total


def mlp_backward(g_all, n_mlp_all, hidden, active, w):
    grad_active = dot(g_all, w["down"], NT)
    density = jnp.exp(-0.5 * hidden * hidden) * 0.3989422804014327
    grad_hidden = (grad_active * (cdf(hidden) + hidden * density)).astype(BF16)
    partial = dot(grad_hidden, w["up"], NT)
    rows = partial.shape[0] // 4
    grad_n_mlp = group_sum([partial[i * rows : (i + 1) * rows] for i in range(4)])
    grad_down = dot(active, g_all, TN).astype(BF16)
    grad_up = dot(n_mlp_all, grad_hidden, TN).astype(BF16)
    grad_b_up = jnp.sum(grad_hidden.astype(F32), axis=0)
    grad_up = place(group_trade(grad_up.reshape(4, -1, grad_up.shape[1])), 1)
    return grad_n_mlp, grad_down, grad_up, grad_b_up


def small_sums(sums, mixed_sums):
    width = sums.shape[1]
    bias = jnp.concatenate([mixed_sums[0, :width], mixed_sums[0, 2 * width :]])
    rest = sums[:5].reshape(5, 4, -1).transpose(1, 0, 2).reshape(4, -1)
    return jnp.concatenate([rest, bias.reshape(4, -1)], axis=1)


def gather_small(stacked):
    names = ("g_attn", "s_attn", "g_mlp", "s_mlp", "b_qv", "b_out", "b_down")
    flat = jnp.concatenate([stacked[name] for name in names], axis=1)
    every = spread(flat, "wt").astype(F32)
    found, at = {}, 0
    for name in names:
        size = stacked[name].shape[1]
        found[name] = every[:, :, at : at + size].transpose(1, 0, 2).reshape(LAYERS, -1)
        at += size
    return found


def local(tokens_in, cotangent, ln_gain_attn, ln_shift_attn, ln_gain_mlp, ln_shift_mlp, w_qkv, b_qv, w_out, b_out, w_up, b_up, w_down, b_down):
    seqs = tokens_in.shape[0]
    width = tokens_in.shape[3]
    rows = seqs * 2 * BLK
    devices = lax.axis_size("ctx")
    depth = width // 4
    unit = b_up.shape[1]
    tables = rotary_tables(seqs)
    small = gather_small(
        {"g_attn": ln_gain_attn, "s_attn": ln_shift_attn, "g_mlp": ln_gain_mlp, "s_mlp": ln_shift_mlp, "b_qv": b_qv, "b_out": b_out, "b_down": b_down}
    )
    half1 = gather_half(w_qkv[0])
    later_out, later_qkv = after((w_out, w_qkv[1]), half1)
    qkv = [gather_rest(half1), lax.all_gather(later_qkv, "wt", axis=0, tiled=True)]
    out_both = lax.all_gather(later_out, "wt", axis=1, tiled=True)
    ups = w_up.reshape(LAYERS * depth, 4, unit).transpose(1, 0, 2)
    ups = exchange(ups, "wt").reshape(4, LAYERS, depth, unit).transpose(1, 0, 2, 3).reshape(LAYERS, width, unit)
    layers = []
    for layer in range(LAYERS):
        w = {name: small[name][layer][None] for name in small}
        w["b_q"] = w["b_qv"][:, :width]
        w["b_v"] = w["b_qv"][:, width:]
        w["qkv"] = qkv[layer]
        w["out"] = out_both[layer]
        w["up"] = ups[layer]
        w["down"] = w_down[layer]
        w["b_up"] = b_up[layer].astype(F32)[None]
        layers.append(w)
    first, second = layers
    g2 = cotangent.reshape(rows, width)
    x1 = tokens_in.reshape(rows, width).astype(F32)
    xhat1, low1, scale1, packed1 = mix(x1, first, tables)
    packed1 = exchange(packed1, "ctx")
    xhat1_all = jnp.concatenate(group_spread(low1), axis=0)
    n_mlp1, hidden1, active1, mlp1 = mlp_forward(xhat1_all, first)
    out1, full1, lse1 = attend(packed1)
    out1 = exchange(out1, "ctx")
    split1, x2 = join(out1, x1, mlp1, first)
    xhat2, low2, scale2, packed2 = mix(x2, second, tables)
    packed2 = exchange(packed2, "ctx")
    grads2 = exchange(pull(g2, second), "ctx")
    xhat2_all = jnp.concatenate(group_spread(low2), axis=0)
    n_mlp2, hidden2, active2, mlp2 = mlp_forward(xhat2_all, second)
    out2, full2, lse2 = attend(packed2)
    back2 = exchange(attend_back(packed2, grads2, full2, lse2), "ctx")
    g2_all = jnp.concatenate(group_spread(g2), axis=0)
    grad_n_mlp2, grad_down2, grad_up2, grad_b_up2 = mlp_backward(g2_all, n_mlp2, hidden2, active2, second)
    mixed2, mixed2_split, mixed_sums2 = unmix(back2, tables)
    g1, g1_low, sums2 = norm_backward(g2.astype(F32), mixed2, grad_n_mlp2, xhat2, scale2, second)
    grads1 = exchange(pull(g1_low, first), "ctx")
    g1_all = jnp.concatenate(group_spread(g1_low), axis=0)
    grad_n_mlp1, grad_down1, grad_up1, grad_b_up1 = mlp_backward(g1_all, n_mlp1, hidden1, active1, first)
    back1 = exchange(attend_back(packed1, grads1, full1, lse1), "ctx")
    out2 = exchange(out2, "ctx")
    split2, x3 = join(out2, x2, mlp2, second)
    out_tokens = x3.astype(BF16).reshape(tokens_in.shape)
    context1_all = jnp.concatenate(group_trade(split1), axis=0)
    context2_all = jnp.concatenate(group_trade(split2), axis=0)
    grad_out2 = dot(context2_all, g2_all, TN).astype(BF16)
    mixed2_all = jnp.concatenate(group_trade(mixed2_split), axis=0)
    grad_out1 = dot(context1_all, g1_all, TN).astype(BF16)
    n_attn2_all = (xhat2_all.astype(F32) * second["g_attn"] + second["s_attn"]).astype(BF16)
    grad_qkv2 = dot(n_attn2_all, mixed2_all, TN).astype(BF16)
    mixed1, mixed1_split, mixed_sums1 = unmix(back1, tables)
    mixed1_all = jnp.concatenate(group_trade(mixed1_split), axis=0)
    n_attn1_all = (xhat1_all.astype(F32) * first["g_attn"] + first["s_attn"]).astype(BF16)
    grad_qkv1 = dot(n_attn1_all, mixed1_all, TN).astype(BF16)
    g0, _, sums1 = norm_backward(g1, mixed1, grad_n_mlp1, xhat1, scale1, first)
    small1, small2 = small_sums(sums1, mixed_sums1), small_sums(sums2, mixed_sums2)
    columns = grad_qkv2.shape[1]
    moved2 = exchange(grad_qkv2.reshape(4, depth, columns), "wt")
    wide = lax.psum((grad_down1, grad_up1, grad_out1, grad_down2, grad_up2, grad_out2, moved2), "ctx")
    smalls, hidden_sums = (small1, small2), (grad_b_up1, grad_b_up2)
    piece = width // devices

    def to_rows(value):
        size = value.shape[-1]
        lines = -(-size // columns)
        lines = -(-lines // 8) * 8
        padded = jnp.pad(value, ((0, 0), (0, lines * columns - size)))
        return padded.reshape(value.shape[0], lines, columns)

    tiny = to_rows(jnp.concatenate(smalls, axis=1).astype(BF16))
    moved = exchange(jnp.concatenate([grad_qkv1.reshape(4, depth, columns), tiny], axis=1), "wt")
    tiny_size = small1.shape[1]
    small_sum = moved[:, depth:].astype(F32).sum(0).reshape(1, -1)[:, : LAYERS * tiny_size]
    tail = to_rows(jnp.concatenate([small_sum, *(u[None] for u in hidden_sums)], axis=1).astype(BF16))
    sent = jnp.concatenate(
        [moved[:, :depth].reshape(devices, piece, columns), jnp.broadcast_to(tail, (devices,) + tail.shape[1:])], axis=1
    )
    landed = exchange(sent, "ctx").astype(F32).sum(0)
    moved1 = spread(landed[:piece].astype(BF16), "ctx").reshape(4, depth, columns)
    flat = landed[piece:].reshape(-1)
    per_layer = [flat[layer * tiny_size : (layer + 1) * tiny_size] for layer in range(LAYERS)]
    at = LAYERS * tiny_size
    grad_b_up = flat[at : at + LAYERS * unit].reshape(LAYERS, unit)

    def vector(index):
        return jnp.stack([v[index * depth : (index + 1) * depth] for v in per_layer])

    def both(one, two):
        return jnp.stack([one.astype(F32), two.astype(F32)])

    grad_bias = vector(4)
    grad_b_qv = jnp.stack([v[5 * depth :] for v in per_layer])
    grad_qkv = both(*(m.transpose(1, 0, 2).reshape(depth, -1) for m in (moved1, wide[6])))
    return (
        out_tokens,
        g0.reshape(tokens_in.shape),
        vector(0),
        vector(1),
        vector(2),
        vector(3),
        grad_qkv,
        grad_b_qv,
        both(wide[2], wide[5]),
        grad_bias,
        both(wide[1], wide[4]),
        grad_b_up,
        both(wide[0], wide[3]),
        grad_bias,
    )


def solution(mesh):
    tokens = P("wt", None, "ctx", None)
    vec, mat = P(None, "wt"), P(None, "wt", None)
    params = (vec, vec, vec, vec, mat, vec, mat, vec, mat, vec, mat, vec)
    return jax.shard_map(
        local,
        mesh=mesh,
        in_specs=(tokens, tokens) + params,
        out_specs=(tokens, tokens) + params,
        check_vma=False,
    )
```

```python
import jax
import jax.numpy as jnp
from jax import lax
from jax.experimental import pallas as pl
from jax.experimental.pallas import tpu as pltpu
from jax.sharding import PartitionSpec as P

HEADS = 12
HEAD_DIM = 64
ROT = 16
LAYERS = 2
BLK = 32
EPS = 1e-05

F32 = jnp.float32
BF16 = jnp.bfloat16
NT = (((1,), (1,)), ((), ()))
NN = (((1,), (0,)), ((), ()))
TILE = 512


def dot(left, right, dims=NN):
    return lax.dot_general(left, right, dims, preferred_element_type=F32)


def exchange(chunks, axis):
    return lax.all_to_all(chunks, axis, 0, 0, tiled=True)


def pass_on(value, shift):
    count = lax.axis_size("wt")
    return lax.ppermute(value, "wt", [(i, (i + shift) % count) for i in range(count)])


def shifts():
    return (1, 3, 2)


def group_spread(value):
    landed = {0: value}
    for shift in shifts():
        landed[shift] = pass_on(value, shift)
    return [landed[shift] for shift in range(4)]


def group_sum(blocks):
    total = blocks[0]
    for shift in shifts():
        total = total + pass_on(blocks[shift].astype(BF16), (4 - shift) % 4).astype(F32)
    return total


def group_trade(chunks):
    here = lax.axis_index("wt")

    def chunk(shift):
        return lax.dynamic_index_in_dim(chunks, (here + shift) % 4, 0, keepdims=False)

    landed = {0: chunk(0)}
    for shift in shifts():
        landed[shift] = pass_on(chunk(shift), shift)
    return [landed[shift] for shift in range(4)]


def place(blocks, axis):
    here = lax.axis_index("wt")
    shape = list(blocks[0].shape)
    size = shape[axis]
    shape[axis] = 4 * size
    whole = jnp.zeros(shape, blocks[0].dtype)
    for shift in range(4):
        whole = lax.dynamic_update_slice_in_dim(whole, blocks[shift], ((here - shift) % 4) * size, axis)
    return whole


def swap(value):
    return lax.ppermute(value, "ctx", [(i, i ^ 1) for i in range(lax.axis_size("ctx"))])


def gather_half(shard):
    core = lax.axis_index("ctx") % 2
    half = shard.shape[0] // 2
    mine = lax.dynamic_slice_in_dim(shard, core * half, half, 0)
    return place([b[None] for b in group_spread(mine)], 0)


def gather_rest(here):
    core = lax.axis_index("ctx") % 2
    other = swap(here)
    first = jnp.where(core == 0, here, other)
    second = jnp.where(core == 0, other, here)
    return jnp.stack([first, second], axis=1).reshape(-1, here.shape[2])


def after(values, first):
    return lax.optimization_barrier((values, first))[0]


def spread(value, axis):
    count = lax.axis_size(axis)
    return exchange(jnp.broadcast_to(value[None], (count,) + value.shape), axis)


def tile_list(size):
    tiles = []
    for start in range(0, size, TILE):
        keys = [(0, k, k == start) for k in range(0, start + TILE, TILE)]
        tiles.append((0, start, keys))
    for start in range(0, size, TILE):
        keys = [(0, k, False) for k in range(0, size, TILE)]
        keys += [(1, k, k == start) for k in range(start, size, TILE)]
        tiles.append((1, start, keys))
    return tiles


def tile_mask(half):
    row = lax.broadcasted_iota(jnp.int32, (TILE, TILE), 0)
    col = lax.broadcasted_iota(jnp.int32, (TILE, TILE), 1)
    if half:
        shift = BLK.bit_length() - 1
        row_pos = (row & (BLK - 1)) - ((row >> shift) << shift)
        col_pos = (col & (BLK - 1)) - ((col >> shift) << shift)
        return row_pos <= col_pos
    return row <= col


def forward_kernel(in_ref, out_ref, full_ref, lse_ref, q_scr, k_scr, vt_scr):
    count = in_ref.shape[0]
    size = count * BLK
    for half in range(2):
        both = in_ref[:, half * BLK : (half + 1) * BLK, :].reshape(size, 128)
        q_scr[half] = both[:, :64] * jnp.asarray(HEAD_DIM ** -0.5, BF16)
        k_scr[half] = both[:, 64:]
    values = in_ref[:, 2 * BLK : 3 * BLK, :].reshape(size, 128)
    vt_scr[...] = values.astype(F32).T.astype(BF16)
    for half, start, keys in tile_list(size):
        query = q_scr[half, start : start + TILE, :]
        top = jnp.full((1, TILE), -1e30, F32)
        total = jnp.zeros((1, TILE), F32)
        acc = jnp.zeros((64, TILE), F32)
        for key_half, key_start, masked in keys:
            key = k_scr[key_half, key_start : key_start + TILE, :]
            scores = dot(key, query, NT)
            if masked:
                scores = jnp.where(tile_mask(half), scores, -1e30)
            new_top = jnp.maximum(top, jnp.max(scores, axis=0, keepdims=True))
            raised = jnp.exp(scores - new_top)
            keep = jnp.exp(top - new_top)
            total = total * keep + jnp.sum(raised, axis=0, keepdims=True)
            value = vt_scr[key_half * 64 : (key_half + 1) * 64, key_start : key_start + TILE]
            acc = acc * keep + dot(value, raised.astype(BF16))
            top = new_top
        full_ref[half * 64 : (half + 1) * 64, start : start + TILE] = acc / total
        lse_ref[half : half + 1, start : start + TILE] = top + jnp.log(total)
    out_ref[...] = full_ref[...].T.astype(BF16).reshape(count, BLK, 128)


def backward_kernel(in_ref, grad_ref, full_ref, lse_ref, carry_ref, out_ref, q_scr, k_scr, kt_scr, v_scr, do_scr, delta_scr, dq_scr, dk_scr, dv_scr):
    count = in_ref.shape[0]
    size = count * BLK
    grads = grad_ref[...].reshape(size, 128)
    grads_t = grads.astype(F32).T
    product = grads_t * full_ref[...]
    values = in_ref[:, 2 * BLK : 3 * BLK, :].reshape(size, 128)
    for half in range(2):
        both = in_ref[:, half * BLK : (half + 1) * BLK, :].reshape(size, 128)
        q_scr[half] = both[:, :64] * jnp.asarray(HEAD_DIM ** -0.5, BF16)
        k_scr[half] = both[:, 64:]
        kt_scr[half] = both.astype(F32).T[64:, :].astype(BF16)
        lanes = slice(half * 64, (half + 1) * 64)
        v_scr[half] = values[:, lanes]
        do_scr[half] = grads[:, lanes]
        delta_scr[half : half + 1, :] = jnp.sum(product[lanes, :], axis=0, keepdims=True)
    dk_scr[...] = jnp.zeros_like(dk_scr)
    dv_scr[...] = jnp.zeros_like(dv_scr)
    for half, start, keys in tile_list(size):
        rows = slice(start, start + TILE)
        query = q_scr[half, rows, :]
        grad = do_scr[half, rows, :]
        lse = lse_ref[half : half + 1, rows]
        delta = delta_scr[half : half + 1, rows]
        acc = jnp.zeros((64, TILE), F32)
        for key_half, key_start, masked in keys:
            key_rows = slice(key_start, key_start + TILE)
            scores = dot(k_scr[key_half, key_rows, :], query, NT)
            if masked:
                scores = jnp.where(tile_mask(half), scores, -1e30)
            probs = jnp.exp(scores - lse)
            grad_probs = dot(v_scr[key_half, key_rows, :], grad, NT)
            grad_scores = (probs * (grad_probs - delta)).astype(BF16)
            dv_scr[key_half, key_rows, :] += dot(probs.astype(BF16), grad)
            dk_scr[key_half, key_rows, :] += dot(grad_scores, query)
            acc += dot(kt_scr[key_half, :, key_rows], grad_scores)
        dq_scr[half * 64 : (half + 1) * 64, rows] = acc * (HEAD_DIM ** -0.5)
    queries = dq_scr[...].T
    for half in range(2):
        both = jnp.concatenate([queries[:, half * 64 : (half + 1) * 64], dk_scr[half]], axis=1)
        out_ref[:, half * BLK : (half + 1) * BLK, :] = both.astype(BF16).reshape(count, BLK, 128)
    if carry_ref.shape[1] > 8:
        out_ref[:, 3 * BLK :, :] = carry_ref[...]
    both = jnp.concatenate([dv_scr[0], dv_scr[1]], axis=1)
    out_ref[:, 2 * BLK : 3 * BLK, :] = both.astype(BF16).reshape(count, BLK, 128)


def attend(packed):
    count = packed.shape[0]
    size = count * BLK
    return pl.pallas_call(
        forward_kernel,
        out_shape=(
            jax.ShapeDtypeStruct((count, BLK, 128), BF16),
            jax.ShapeDtypeStruct((128, size), F32),
            jax.ShapeDtypeStruct((8, size), F32),
        ),
        in_specs=[pl.BlockSpec(memory_space=pltpu.VMEM)],
        out_specs=[pl.BlockSpec(memory_space=pltpu.VMEM)] * 3,
        scratch_shapes=[
            pltpu.VMEM((2, size, 64), BF16),
            pltpu.VMEM((2, size, 64), BF16),
            pltpu.VMEM((128, size), BF16),
        ],
        compiler_params=pltpu.CompilerParams(vmem_limit_bytes=48 << 20),
        cost_estimate=pl.CostEstimate(flops=20_000_000_000, bytes_accessed=20_000_000, transcendentals=2_600_000),
        name="attend",
    )(packed)


def attend_back(packed, grads, full, lse, carry):
    extra = carry.shape[1] if carry.shape[1] > 8 else 0
    count = packed.shape[0]
    size = count * BLK
    return pl.pallas_call(
        backward_kernel,
        out_shape=jax.ShapeDtypeStruct((count, 3 * BLK + extra, 128), BF16),
        in_specs=[pl.BlockSpec(memory_space=pltpu.VMEM)] * 5,
        out_specs=pl.BlockSpec(memory_space=pltpu.VMEM),
        scratch_shapes=[
            pltpu.VMEM((2, size, 64), BF16),
            pltpu.VMEM((2, size, 64), BF16),
            pltpu.VMEM((2, 64, size), BF16),
            pltpu.VMEM((2, size, 64), BF16),
            pltpu.VMEM((2, size, 64), BF16),
            pltpu.VMEM((8, size), F32),
            pltpu.VMEM((128, size), F32),
            pltpu.VMEM((2, size, 64), F32),
            pltpu.VMEM((2, size, 64), F32),
        ],
        compiler_params=pltpu.CompilerParams(vmem_limit_bytes=48 << 20),
        cost_estimate=pl.CostEstimate(flops=40_000_000_000, bytes_accessed=40_000_000, transcendentals=2_600_000),
        name="attend_back",
    )(packed, grads, full, lse, carry)


def kernel_turn(value, tables, sign):
    cosine, up, down = tables
    half = ROT // 2
    back = value.shape[1] - half
    turned = pltpu.roll(value, half, 1) * up - pltpu.roll(value, back, 1) * down
    return value * cosine + sign * turned


def head(value, rows, index):
    return value[rows, index * HEAD_DIM : (index + 1) * HEAD_DIM]


def mix_kernel(x_ref, gain_ref, shift_ref, w_ref, bq_ref, bv_ref, cos_ref, up_ref, down_ref, extra_ref, xhat_ref, send_ref, scale_ref, out_ref):
    x = x_ref[...]
    rows, width = x.shape
    centred = x - jnp.mean(x, axis=-1, keepdims=True)
    scale = lax.rsqrt(jnp.mean(centred * centred, axis=-1, keepdims=True) + EPS)
    xhat = centred * scale
    xhat_ref[...] = xhat
    for block in range(send_ref.shape[0]):
        send_ref[block, :, :width] = xhat.astype(BF16)
        send_ref[block, :, width:] = extra_ref[block]
    scale_ref[...] = jnp.broadcast_to(scale, scale_ref.shape)
    normed = (xhat * gain_ref[...] + shift_ref[...]).astype(BF16)
    tables = (cos_ref[...], up_ref[...], down_ref[...])
    query = kernel_turn(dot(normed, w_ref[:, :width]) + bq_ref[...], tables, 1.0)
    key = kernel_turn(dot(normed, w_ref[:, width : 2 * width]), tables, 1.0)
    value = dot(normed, w_ref[:, 2 * width :]) + bv_ref[...]
    seqs = rows // (2 * BLK)
    for s in range(seqs):
        at = s * 2 * BLK
        whole, early, late = slice(at, at + 2 * BLK), slice(at, at + BLK), slice(at + BLK, at + 2 * BLK)
        for h in range(HEADS):
            pair = jnp.concatenate([head(query, whole, h), head(key, whole, h)], axis=1)
            out_ref[s * HEADS + h, : 2 * BLK, :] = pair.astype(BF16)
            pair = jnp.concatenate([head(value, early, h), head(value, late, h)], axis=1)
            out_ref[s * HEADS + h, 2 * BLK :, :] = pair.astype(BF16)
    spare = out_ref.shape[0] - seqs * HEADS
    out_ref[seqs * HEADS :, :, :] = jnp.zeros((spare,) + out_ref.shape[1:], BF16)


def on_chip(kernel, out_shape, name, flops, *operands, scratch=()):
    many = isinstance(out_shape, tuple)
    spec = pl.BlockSpec(memory_space=pltpu.VMEM)
    return pl.pallas_call(
        kernel,
        out_shape=out_shape,
        in_specs=[spec] * len(operands),
        out_specs=[spec] * len(out_shape) if many else spec,
        scratch_shapes=list(scratch),
        compiler_params=pltpu.CompilerParams(vmem_limit_bytes=48 << 20),
        cost_estimate=pl.CostEstimate(flops=flops, bytes_accessed=8_000_000, transcendentals=0),
        name=name,
    )(*operands)


def shaped(shape, dtype):
    return jax.ShapeDtypeStruct(shape, dtype)


def mix(x, w, tables, extra):
    rows, width = x.shape
    count = lax.axis_size("ctx")
    shapes = (
        shaped((rows, width), F32),
        shaped((extra.shape[0], rows, width + extra.shape[2]), BF16),
        shaped((rows, 128), F32),
        shaped((count, 3 * BLK, 128), BF16),
    )
    return on_chip(mix_kernel, shapes, "mix", 5_000_000_000, x, w["g_attn"], w["s_attn"], w["qkv"], w["b_q"], w["b_v"], *tables, extra)


def join_kernel(tile_ref, x_ref, mlp_ref, w_ref, bias_ref, split_ref, out_ref, context):
    rows, width = context.shape
    for s in range(rows // (2 * BLK)):
        for half in range(2):
            at = (2 * s + half) * BLK
            lanes = slice(half * HEAD_DIM, (half + 1) * HEAD_DIM)
            row = [tile_ref[s * HEADS + h, :, lanes] for h in range(HEADS)]
            context[at : at + BLK, :] = jnp.concatenate(row, axis=1)
    size = width // 4
    for block in range(4):
        split_ref[block] = context[:, block * size : (block + 1) * size]
    out_ref[...] = x_ref[...] + dot(context[...], w_ref[...]) + (mlp_ref[...] + bias_ref[...])


def join(tiles, x, mlp, w):
    rows, width = x.shape
    shapes = (shaped((4, rows, width // 4), BF16), shaped((rows, width), F32))
    scratch = [pltpu.VMEM((rows, width), BF16)]
    return on_chip(join_kernel, shapes, "join", 500_000_000, tiles, x, mlp, w["out"], w["b_out"] + w["b_down"], scratch=scratch)


def pull_kernel(g_ref, w_ref, out_ref):
    grad = dot(g_ref[...], w_ref[...], NT)
    seqs = grad.shape[0] // (2 * BLK)
    for s in range(seqs):
        at = s * 2 * BLK
        for h in range(HEADS):
            early, late = head(grad, slice(at, at + BLK), h), head(grad, slice(at + BLK, at + 2 * BLK), h)
            out_ref[s * HEADS + h] = jnp.concatenate([early, late], axis=1).astype(BF16)
    spare = out_ref.shape[0] - seqs * HEADS
    out_ref[seqs * HEADS :, :, :] = jnp.zeros((spare,) + out_ref.shape[1:], BF16)


def pull(g_low, w):
    count = lax.axis_size("ctx")
    return on_chip(pull_kernel, shaped((count, BLK, 128), BF16), "pull", 500_000_000, g_low, w["out"])


def unmix_kernel(tile_ref, cos_ref, up_ref, down_ref, mixed_ref, split_ref, sums_ref):
    rows, width = cos_ref.shape
    tables = (cos_ref[...], up_ref[...], down_ref[...])
    parts = [[], [], []]
    for s in range(rows // (2 * BLK)):
        for part in range(2):
            lanes = slice(part * HEAD_DIM, (part + 1) * HEAD_DIM)
            row = [tile_ref[s * HEADS + h, : 2 * BLK, lanes] for h in range(HEADS)]
            parts[part].append(jnp.concatenate(row, axis=1))
        for half in range(2):
            lanes = slice(half * HEAD_DIM, (half + 1) * HEAD_DIM)
            row = [tile_ref[s * HEADS + h, 2 * BLK : 3 * BLK, lanes] for h in range(HEADS)]
            parts[2].append(jnp.concatenate(row, axis=1))
    query, key, value = (jnp.concatenate(part, axis=0) for part in parts)
    mixed_ref[:, :width] = kernel_turn(query.astype(F32), tables, -1.0).astype(BF16)
    mixed_ref[:, width : 2 * width] = kernel_turn(key.astype(F32), tables, -1.0).astype(BF16)
    mixed_ref[:, 2 * width :] = value
    size = 3 * width // 4
    for block in range(4):
        split_ref[block] = mixed_ref[:, block * size : (block + 1) * size]
    sums_ref[...] = jnp.sum(mixed_ref[...].astype(F32), axis=0, keepdims=True)


def unmix(tiles, tables):
    rows, width = tables[0].shape
    shapes = (
        shaped((rows, 3 * width), BF16),
        shaped((4, rows, 3 * width // 4), BF16),
        shaped((1, 3 * width), F32),
    )
    return on_chip(unmix_kernel, shapes, "unmix", 500_000_000, tiles, *tables)


def norm_kernel(mixed_ref, w_ref, g_ref, mlp_ref, xhat_ref, scale_ref, ga_ref, gm_ref, split_ref, context_ref, out_ref, low_ref, send_ref, sums_ref):
    attn = dot(mixed_ref[...], w_ref[...], NT)
    mlp, xhat, g = mlp_ref[...], xhat_ref[...], g_ref[...]
    both = attn * ga_ref[...] + mlp * gm_ref[...]
    inner = both - jnp.mean(both, axis=-1, keepdims=True) - xhat * jnp.mean(both * xhat, axis=-1, keepdims=True)
    new = g + scale_ref[:, :1] * inner
    out_ref[...] = new
    low_ref[...] = new.astype(BF16)
    if send_ref.shape[0] == 4:
        width = new.shape[1]
        size, rest = split_ref.shape[2], context_ref.shape[2]
        send_ref[...] = jnp.zeros_like(send_ref)
        for block in range(4):
            send_ref[block, :, :width] = new.astype(BF16)
            send_ref[block, :, width : width + size] = split_ref[block]
            send_ref[block, :, send_ref.shape[2] - rest :] = context_ref[block]
    sums_ref[...] = jnp.zeros_like(sums_ref)
    for row, value in enumerate((attn * xhat, attn, mlp * xhat, mlp, g.astype(BF16).astype(F32))):
        sums_ref[row : row + 1, :] = jnp.sum(value, axis=0, keepdims=True)


def norm_backward(g, mixed, grad_n_mlp, xhat, scale, w, split, context, send):
    rows, width = g.shape
    size = -(-split.shape[2] // 128) * 128
    sent = (4, rows, width + size + context.shape[2]) if send else (1, 8, 128)
    shapes = (shaped((rows, width), F32), shaped((rows, width), BF16), shaped(sent, BF16), shaped((8, width), F32))
    return on_chip(
        norm_kernel, shapes, "norm_back", 1_500_000_000, mixed, w["qkv"], g, grad_n_mlp, xhat, scale, w["g_attn"], w["g_mlp"], split, context
    )


def rotary_tables(seqs):
    device = lax.axis_index("ctx")
    devices = lax.axis_size("ctx")
    offsets = jnp.arange(BLK, dtype=jnp.int32)
    early = device * BLK + offsets
    late = 2 * BLK * devices - (device + 1) * BLK + offsets
    positions = jnp.tile(jnp.concatenate([early, late]), seqs).astype(F32)
    half = ROT // 2
    frequency = 10000.0 ** (-jnp.arange(half, dtype=F32) * 2.0 / ROT)
    angles = positions[:, None] * frequency[None, :]
    cosine, sine = lax.optimization_barrier((jnp.cos(angles), jnp.sin(angles)))
    rows = positions.shape[0]
    zero = jnp.zeros((rows, half), F32)
    rest = HEAD_DIM - ROT

    def whole(first, second, fill):
        return jnp.tile(jnp.concatenate([first, second, jnp.full((rows, rest), fill, F32)], axis=1), (1, HEADS))

    tables = (whole(cosine, cosine, 1.0), whole(zero, sine, 0.0), whole(sine, zero, 0.0))
    return lax.optimization_barrier(tables)


def cdf(value):
    return 0.5 * (1.0 + lax.erf(value * (0.5 ** 0.5)))


TN = (((0,), (0,)), ((), ()))


def split_columns(value):
    return value.reshape(value.shape[0], 4, -1).transpose(1, 0, 2)


def mlp_forward(xhat_all, w):
    n_mlp_all = (xhat_all.astype(F32) * w["g_mlp"] + w["s_mlp"]).astype(BF16)
    hidden = dot(n_mlp_all, w["up"]) + w["b_up"]
    active = (hidden * cdf(hidden)).astype(BF16)
    return n_mlp_all, hidden, active, dot(active, w["down"])


def own_sum(partial):
    rows = partial.shape[0] // 4
    return group_sum([partial[i * rows : (i + 1) * rows] for i in range(4)])


def mlp_backward(g_all, n_mlp_all, hidden, active, w):
    grad_active = dot(g_all, w["down"], NT)
    density = jnp.exp(-0.5 * hidden * hidden) * 0.3989422804014327
    grad_hidden = (grad_active * (cdf(hidden) + hidden * density)).astype(BF16)
    partial = dot(grad_hidden, w["up"], NT)
    grad_down = dot(active, g_all, TN).astype(BF16)
    grad_up = dot(n_mlp_all, grad_hidden, TN).astype(BF16)
    grad_b_up = jnp.sum(grad_hidden.astype(F32), axis=0)
    return partial, grad_down, grad_up.reshape(4, -1, grad_up.shape[1]), grad_b_up


def small_sums(sums, mixed_sums):
    width = sums.shape[1]
    bias = jnp.concatenate([mixed_sums[0, :width], mixed_sums[0, 2 * width :]])
    rest = sums[:5].reshape(5, 4, -1).transpose(1, 0, 2).reshape(4, -1)
    return jnp.concatenate([rest, bias.reshape(4, -1)], axis=1)


def gather_small(stacked):
    names = ("g_attn", "s_attn", "g_mlp", "s_mlp", "b_qv", "b_out", "b_down")
    flat = jnp.concatenate([stacked[name] for name in names], axis=1)
    every = spread(flat, "wt").astype(F32)
    found, at = {}, 0
    for name in names:
        size = stacked[name].shape[1]
        found[name] = every[:, :, at : at + size].transpose(1, 0, 2).reshape(LAYERS, -1)
        at += size
    return found


def local(tokens_in, cotangent, ln_gain_attn, ln_shift_attn, ln_gain_mlp, ln_shift_mlp, w_qkv, b_qv, w_out, b_out, w_up, b_up, w_down, b_down):
    seqs = tokens_in.shape[0]
    width = tokens_in.shape[3]
    rows = seqs * 2 * BLK
    devices = lax.axis_size("ctx")
    depth = width // 4
    unit = b_up.shape[1]
    tables = rotary_tables(seqs)
    small = gather_small(
        {"g_attn": ln_gain_attn, "s_attn": ln_shift_attn, "g_mlp": ln_gain_mlp, "s_mlp": ln_shift_mlp, "b_qv": b_qv, "b_out": b_out, "b_down": b_down}
    )
    half1 = gather_half(w_qkv[0])
    later_out, later_qkv, later_up = after((w_out, w_qkv[1], w_up), half1)
    qkv = [gather_rest(half1), lax.all_gather(later_qkv, "wt", axis=0, tiled=True)]
    out_both = lax.all_gather(later_out, "wt", axis=1, tiled=True)
    ups = jnp.stack([later_up[:, :, i * unit : (i + 1) * unit] for i in range(4)])
    ups = place([b[:, None] for b in group_trade(ups)], 1).reshape(LAYERS, width, unit)
    layers = []
    for layer in range(LAYERS):
        w = {name: small[name][layer][None] for name in small}
        w["b_q"] = w["b_qv"][:, :width]
        w["b_v"] = w["b_qv"][:, width:]
        w["qkv"] = qkv[layer]
        w["out"] = out_both[layer]
        w["up"] = ups[layer]
        w["down"] = w_down[layer]
        w["b_up"] = b_up[layer].astype(F32)[None]
        layers.append(w)
    first, second = layers
    g2 = cotangent.reshape(rows, width)
    x1 = tokens_in.reshape(rows, width).astype(F32)
    xhat1, send1, scale1, packed1 = mix(x1, first, tables, g2[None])
    packed1 = exchange(packed1, "ctx")
    landed1 = jnp.concatenate(group_spread(send1[0]), axis=0)
    xhat1_all, g2_all = landed1[:, :width], landed1[:, width:]
    n_mlp1, hidden1, active1, partial1 = mlp_forward(xhat1_all, first)
    mlp1 = own_sum(partial1)
    out1, full1, lse1 = attend(packed1)
    both1 = exchange(jnp.concatenate([out1, pull(g2, second)], axis=1), "ctx")
    out1, grads2 = both1[:, :BLK], both1[:, BLK:]
    split1, x2 = join(out1, x1, mlp1, first)
    xhat2, send2, scale2, packed2 = mix(x2, second, tables, split1)
    packed2 = exchange(packed2, "ctx")
    landed2 = jnp.concatenate(group_trade(send2), axis=0)
    xhat2_all, context1_all = landed2[:, :width], landed2[:, width:]
    n_mlp2, hidden2, active2, partial2 = mlp_forward(xhat2_all, second)
    out2, full2, lse2 = attend(packed2)
    back2 = exchange(attend_back(packed2, grads2, full2, lse2, out2), "ctx")
    back_partial2, grad_down2, grad_up2, grad_b_up2 = mlp_backward(g2_all, n_mlp2, hidden2, active2, second)
    sums = own_sum(jnp.concatenate([partial2, back_partial2], axis=1))
    mlp2, grad_n_mlp2 = sums[:, :width], sums[:, width:]
    split2, x3 = join(back2[:, 3 * BLK :], x2, mlp2, second)
    out_tokens = x3.astype(BF16).reshape(tokens_in.shape)
    mixed2, mixed2_split, mixed_sums2 = unmix(back2, tables)
    g1, g1_low, send3, sums2 = norm_backward(g2.astype(F32), mixed2, grad_n_mlp2, xhat2, scale2, second, mixed2_split, split2, True)
    grads1 = exchange(pull(g1_low, first), "ctx")
    landed3 = jnp.concatenate(group_trade(send3), axis=0)
    columns = mixed2_split.shape[2]
    g1_all, mixed2_all, context2_all = landed3[:, :width], landed3[:, width : width + columns], landed3[:, -depth:]
    back_partial1, grad_down1, grad_up1, grad_b_up1 = mlp_backward(g1_all, n_mlp1, hidden1, active1, first)
    grad_n_mlp1 = own_sum(back_partial1)
    back1 = exchange(attend_back(packed1, grads1, full1, lse1, lse1[None].astype(BF16)), "ctx")
    grad_up1 = place([b[None] for b in group_trade(grad_up1)], 0).reshape(width, unit)
    grad_out1 = dot(context1_all, g1_all, TN).astype(BF16)
    grad_out2 = dot(context2_all, g2_all, TN).astype(BF16)
    n_attn2_all = (xhat2_all.astype(F32) * second["g_attn"] + second["s_attn"]).astype(BF16)
    grad_qkv2 = dot(n_attn2_all, mixed2_all, TN).astype(BF16)
    traded2 = group_trade(jnp.concatenate([grad_up2, grad_qkv2.reshape(4, depth, columns)], axis=2))
    space = jnp.zeros((width, width - columns), BF16)
    parts2 = [grad_down2, grad_out2] + [b[:, :unit] for b in traded2]
    tall2 = jnp.concatenate(parts2 + [jnp.concatenate([jnp.concatenate([b[:, unit:] for b in traded2], axis=0), space], axis=1)], axis=0)
    back1, tall2 = lax.optimization_barrier((back1, tall2))
    tall2 = lax.psum_scatter(tall2.reshape(devices, -1, width), "ctx", scatter_dimension=0, tiled=False)
    wide1 = jnp.concatenate([grad_down1, grad_up1, grad_out1], axis=0)
    wide1 = exchange(wide1.reshape(devices, -1, width), "ctx").astype(F32).sum(0).astype(BF16)
    mixed1, mixed1_split, mixed_sums1 = unmix(back1, tables)
    mixed1_all = jnp.concatenate(group_trade(mixed1_split), axis=0)
    n_attn1_all = (xhat1_all.astype(F32) * first["g_attn"] + first["s_attn"]).astype(BF16)
    grad_qkv1 = dot(n_attn1_all, mixed1_all, TN).astype(BF16)
    g0, _, _, sums1 = norm_backward(g1, mixed1, grad_n_mlp1, xhat1, scale1, first, mixed2_split, split2, False)
    small1, small2 = small_sums(sums1, mixed_sums1), small_sums(sums2, mixed_sums2)
    smalls, hidden_sums = (small1, small2), (grad_b_up1, grad_b_up2)
    piece = width // devices

    def to_rows(value):
        size = value.shape[-1]
        lines = -(-size // columns)
        lines = -(-lines // 8) * 8
        padded = jnp.pad(value, ((0, 0), (0, lines * columns - size)))
        return padded.reshape(value.shape[0], lines, columns)

    tiny = to_rows(jnp.concatenate(smalls, axis=1).astype(BF16))
    moved = group_trade(jnp.concatenate([grad_qkv1.reshape(4, depth, columns), tiny], axis=1))
    moved = place([b[None] for b in moved], 0)
    tiny_size = small1.shape[1]
    small_sum = moved[:, depth:].astype(F32).sum(0).reshape(1, -1)[:, : LAYERS * tiny_size]
    tail = to_rows(jnp.concatenate([small_sum, *(u[None] for u in hidden_sums)], axis=1).astype(BF16))
    sent = jnp.concatenate(
        [moved[:, :depth].reshape(devices, piece, columns), jnp.broadcast_to(tail, (devices,) + tail.shape[1:])], axis=1
    )
    landed = exchange(after(sent, wide1), "ctx").astype(F32).sum(0)
    lines = wide1.shape[0]
    tall2 = after(tall2, landed)
    tall2 = lax.all_gather(tall2, "ctx", axis=0).reshape(-1, width)
    wide2 = (tall2[:unit], tall2[unit : unit + depth])
    traded_up2 = tall2[unit + depth : unit + depth + width].reshape(4, depth, unit)
    traded_qkv2 = tall2[unit + depth + width :, :columns].reshape(4, depth, columns)
    last = jnp.pad(landed[:piece].astype(BF16), ((0, 0), (0, width - columns)))
    last = spread(jnp.concatenate([wide1, last], axis=0), "ctx")
    wide1 = last[:, :lines].reshape(-1, width)
    moved1 = last[:, lines:, :columns].reshape(4, depth, columns)
    up1 = wide1[unit : unit + width].reshape(4, depth, unit)
    up2 = place([traded_up2[i : i + 1] for i in range(4)], 0)
    qkv2 = place([traded_qkv2[i : i + 1] for i in range(4)], 0)

    def side_by_side(blocks):
        return blocks.transpose(1, 0, 2).reshape(depth, -1)

    flat = landed[piece:].reshape(-1)
    per_layer = [flat[layer * tiny_size : (layer + 1) * tiny_size] for layer in range(LAYERS)]
    at = LAYERS * tiny_size
    grad_b_up = flat[at : at + LAYERS * unit].reshape(LAYERS, unit)

    def vector(index):
        return jnp.stack([v[index * depth : (index + 1) * depth] for v in per_layer])

    def both(one, two):
        return jnp.stack([one.astype(F32), two.astype(F32)])

    grad_bias = vector(4)
    grad_b_qv = jnp.stack([v[5 * depth :] for v in per_layer])
    grad_qkv = both(side_by_side(moved1), side_by_side(qkv2))
    return (
        out_tokens,
        g0.reshape(tokens_in.shape),
        vector(0),
        vector(1),
        vector(2),
        vector(3),
        grad_qkv,
        grad_b_qv,
        both(wide1[unit + width :], wide2[1]),
        grad_bias,
        both(side_by_side(up1), side_by_side(up2)),
        grad_b_up,
        both(wide1[:unit], wide2[0]),
        grad_bias,
    )


def solution(mesh):
    tokens = P("wt", None, "ctx", None)
    vec, mat = P(None, "wt"), P(None, "wt", None)
    params = (vec, vec, vec, vec, mat, vec, mat, vec, mat, vec, mat, vec)
    return jax.shard_map(
        local,
        mesh=mesh,
        in_specs=(tokens, tokens) + params,
        out_specs=(tokens, tokens) + params,
        check_vma=False,
    )
```

```python
import jax
import jax.numpy as jnp
from jax import lax
from jax.experimental import pallas as pl
from jax.experimental.pallas import tpu as pltpu
from jax.sharding import PartitionSpec as P

HEADS = 12
HEAD_DIM = 64
ROT = 16
LAYERS = 2
BLK = 32
EPS = 1e-05

F32 = jnp.float32
BF16 = jnp.bfloat16
NT = (((1,), (1,)), ((), ()))
NN = (((1,), (0,)), ((), ()))
TILE = 512


def dot(left, right, dims=NN):
    return lax.dot_general(left, right, dims, preferred_element_type=F32)


def exchange(chunks, axis):
    return lax.all_to_all(chunks, axis, 0, 0, tiled=True)


def pass_on(value, shift):
    count = lax.axis_size("wt")
    return lax.ppermute(value, "wt", [(i, (i + shift) % count) for i in range(count)])


def shifts():
    return (1, 3, 2)


def group_spread(value):
    landed = {0: value}
    for shift in shifts():
        landed[shift] = pass_on(value, shift)
    return [landed[shift] for shift in range(4)]


def group_sum(blocks):
    total = blocks[0]
    for shift in shifts():
        total = total + pass_on(blocks[shift].astype(BF16), (4 - shift) % 4).astype(F32)
    return total


def group_trade(chunks):
    here = lax.axis_index("wt")

    def chunk(shift):
        return lax.dynamic_index_in_dim(chunks, (here + shift) % 4, 0, keepdims=False)

    landed = {0: chunk(0)}
    for shift in shifts():
        landed[shift] = pass_on(chunk(shift), shift)
    return [landed[shift] for shift in range(4)]


def place(blocks, axis):
    here = lax.axis_index("wt")
    shape = list(blocks[0].shape)
    size = shape[axis]
    shape[axis] = 4 * size
    whole = jnp.zeros(shape, blocks[0].dtype)
    for shift in range(4):
        whole = lax.dynamic_update_slice_in_dim(whole, blocks[shift], ((here - shift) % 4) * size, axis)
    return whole


def swap(value):
    return lax.ppermute(value, "ctx", [(i, i ^ 1) for i in range(lax.axis_size("ctx"))])


def gather_half(shard):
    core = lax.axis_index("ctx") % 2
    half = shard.shape[0] // 2
    mine = lax.dynamic_slice_in_dim(shard, core * half, half, 0)
    return place([b[None] for b in group_spread(mine)], 0)


def gather_rest(here):
    core = lax.axis_index("ctx") % 2
    other = swap(here)
    first = jnp.where(core == 0, here, other)
    second = jnp.where(core == 0, other, here)
    return jnp.stack([first, second], axis=1).reshape(-1, here.shape[2])


def after(values, first):
    return lax.optimization_barrier((values, first))[0]


def spread(value, axis):
    count = lax.axis_size(axis)
    return exchange(jnp.broadcast_to(value[None], (count,) + value.shape), axis)


def tile_list(size):
    tiles = []
    for start in range(0, size, TILE):
        keys = [(0, k, k == start) for k in range(0, start + TILE, TILE)]
        tiles.append((0, start, keys))
    for start in range(0, size, TILE):
        keys = [(0, k, False) for k in range(0, size, TILE)]
        keys += [(1, k, k == start) for k in range(start, size, TILE)]
        tiles.append((1, start, keys))
    return tiles


def tile_mask(half):
    row = lax.broadcasted_iota(jnp.int32, (TILE, TILE), 0)
    col = lax.broadcasted_iota(jnp.int32, (TILE, TILE), 1)
    if half:
        shift = BLK.bit_length() - 1
        row_pos = (row & (BLK - 1)) - ((row >> shift) << shift)
        col_pos = (col & (BLK - 1)) - ((col >> shift) << shift)
        return row_pos <= col_pos
    return row <= col


def forward_kernel(in_ref, out_ref, full_ref, lse_ref, q_scr, k_scr, vt_scr):
    count = in_ref.shape[0]
    size = count * BLK
    for half in range(2):
        both = in_ref[:, half * BLK : (half + 1) * BLK, :].reshape(size, 128)
        q_scr[half] = both[:, :64] * jnp.asarray(HEAD_DIM ** -0.5, BF16)
        k_scr[half] = both[:, 64:]
    values = in_ref[:, 2 * BLK : 3 * BLK, :].reshape(size, 128)
    vt_scr[...] = values.astype(F32).T.astype(BF16)
    for half, start, keys in tile_list(size):
        query = q_scr[half, start : start + TILE, :]
        top = jnp.full((1, TILE), -1e30, F32)
        total = jnp.zeros((1, TILE), F32)
        acc = jnp.zeros((64, TILE), F32)
        for key_half, key_start, masked in keys:
            key = k_scr[key_half, key_start : key_start + TILE, :]
            scores = dot(key, query, NT)
            if masked:
                scores = jnp.where(tile_mask(half), scores, -1e30)
            new_top = jnp.maximum(top, jnp.max(scores, axis=0, keepdims=True))
            raised = jnp.exp(scores - new_top)
            keep = jnp.exp(top - new_top)
            total = total * keep + jnp.sum(raised, axis=0, keepdims=True)
            value = vt_scr[key_half * 64 : (key_half + 1) * 64, key_start : key_start + TILE]
            acc = acc * keep + dot(value, raised.astype(BF16))
            top = new_top
        full_ref[half * 64 : (half + 1) * 64, start : start + TILE] = acc / total
        lse_ref[half : half + 1, start : start + TILE] = top + jnp.log(total)
    out_ref[...] = full_ref[...].T.astype(BF16).reshape(count, BLK, 128)


def backward_kernel(in_ref, grad_ref, full_ref, lse_ref, carry_ref, out_ref, q_scr, k_scr, kt_scr, v_scr, do_scr, delta_scr, dq_scr, dk_scr, dv_scr):
    count = in_ref.shape[0]
    size = count * BLK
    grads = grad_ref[...].reshape(size, 128)
    grads_t = grads.astype(F32).T
    product = grads_t * full_ref[...]
    values = in_ref[:, 2 * BLK : 3 * BLK, :].reshape(size, 128)
    for half in range(2):
        both = in_ref[:, half * BLK : (half + 1) * BLK, :].reshape(size, 128)
        q_scr[half] = both[:, :64] * jnp.asarray(HEAD_DIM ** -0.5, BF16)
        k_scr[half] = both[:, 64:]
        kt_scr[half] = both.astype(F32).T[64:, :].astype(BF16)
        lanes = slice(half * 64, (half + 1) * 64)
        v_scr[half] = values[:, lanes]
        do_scr[half] = grads[:, lanes]
        delta_scr[half : half + 1, :] = jnp.sum(product[lanes, :], axis=0, keepdims=True)
    dk_scr[...] = jnp.zeros_like(dk_scr)
    dv_scr[...] = jnp.zeros_like(dv_scr)
    for half, start, keys in tile_list(size):
        rows = slice(start, start + TILE)
        query = q_scr[half, rows, :]
        grad = do_scr[half, rows, :]
        lse = lse_ref[half : half + 1, rows]
        delta = delta_scr[half : half + 1, rows]
        acc = jnp.zeros((64, TILE), F32)
        for key_half, key_start, masked in keys:
            key_rows = slice(key_start, key_start + TILE)
            scores = dot(k_scr[key_half, key_rows, :], query, NT)
            if masked:
                scores = jnp.where(tile_mask(half), scores, -1e30)
            probs = jnp.exp(scores - lse)
            grad_probs = dot(v_scr[key_half, key_rows, :], grad, NT)
            grad_scores = (probs * (grad_probs - delta)).astype(BF16)
            dv_scr[key_half, key_rows, :] += dot(probs.astype(BF16), grad)
            dk_scr[key_half, key_rows, :] += dot(grad_scores, query)
            acc += dot(kt_scr[key_half, :, key_rows], grad_scores)
        dq_scr[half * 64 : (half + 1) * 64, rows] = acc * (HEAD_DIM ** -0.5)
    queries = dq_scr[...].T
    for half in range(2):
        both = jnp.concatenate([queries[:, half * 64 : (half + 1) * 64], dk_scr[half]], axis=1)
        out_ref[:, half * BLK : (half + 1) * BLK, :] = both.astype(BF16).reshape(count, BLK, 128)
    if carry_ref.shape[1] > 8:
        out_ref[:, 3 * BLK :, :] = carry_ref[...]
    both = jnp.concatenate([dv_scr[0], dv_scr[1]], axis=1)
    out_ref[:, 2 * BLK : 3 * BLK, :] = both.astype(BF16).reshape(count, BLK, 128)


def attend(packed):
    count = packed.shape[0]
    size = count * BLK
    return pl.pallas_call(
        forward_kernel,
        out_shape=(
            jax.ShapeDtypeStruct((count, BLK, 128), BF16),
            jax.ShapeDtypeStruct((128, size), F32),
            jax.ShapeDtypeStruct((8, size), F32),
        ),
        in_specs=[pl.BlockSpec(memory_space=pltpu.VMEM)],
        out_specs=[pl.BlockSpec(memory_space=pltpu.VMEM)] * 3,
        scratch_shapes=[
            pltpu.VMEM((2, size, 64), BF16),
            pltpu.VMEM((2, size, 64), BF16),
            pltpu.VMEM((128, size), BF16),
        ],
        compiler_params=pltpu.CompilerParams(vmem_limit_bytes=48 << 20),
        cost_estimate=pl.CostEstimate(flops=20_000_000_000, bytes_accessed=20_000_000, transcendentals=2_600_000),
        name="attend",
    )(packed)


def attend_back(packed, grads, full, lse, carry):
    extra = carry.shape[1] if carry.shape[1] > 8 else 0
    count = packed.shape[0]
    size = count * BLK
    return pl.pallas_call(
        backward_kernel,
        out_shape=jax.ShapeDtypeStruct((count, 3 * BLK + extra, 128), BF16),
        in_specs=[pl.BlockSpec(memory_space=pltpu.VMEM)] * 5,
        out_specs=pl.BlockSpec(memory_space=pltpu.VMEM),
        scratch_shapes=[
            pltpu.VMEM((2, size, 64), BF16),
            pltpu.VMEM((2, size, 64), BF16),
            pltpu.VMEM((2, 64, size), BF16),
            pltpu.VMEM((2, size, 64), BF16),
            pltpu.VMEM((2, size, 64), BF16),
            pltpu.VMEM((8, size), F32),
            pltpu.VMEM((128, size), F32),
            pltpu.VMEM((2, size, 64), F32),
            pltpu.VMEM((2, size, 64), F32),
        ],
        compiler_params=pltpu.CompilerParams(vmem_limit_bytes=48 << 20),
        cost_estimate=pl.CostEstimate(flops=40_000_000_000, bytes_accessed=40_000_000, transcendentals=2_600_000),
        name="attend_back",
    )(packed, grads, full, lse, carry)


def kernel_turn(value, tables, sign):
    cosine, up, down = tables
    half = ROT // 2
    back = value.shape[1] - half
    turned = pltpu.roll(value, half, 1) * up - pltpu.roll(value, back, 1) * down
    return value * cosine + sign * turned


def head(value, rows, index):
    return value[rows, index * HEAD_DIM : (index + 1) * HEAD_DIM]


def mix_kernel(x_ref, gain_ref, shift_ref, w_ref, bq_ref, bv_ref, cos_ref, up_ref, down_ref, extra_ref, xhat_ref, send_ref, scale_ref, out_ref):
    x = x_ref[...]
    rows, width = x.shape
    centred = x - jnp.mean(x, axis=-1, keepdims=True)
    scale = lax.rsqrt(jnp.mean(centred * centred, axis=-1, keepdims=True) + EPS)
    xhat = centred * scale
    xhat_ref[...] = xhat
    for block in range(send_ref.shape[0]):
        send_ref[block, :, :width] = xhat.astype(BF16)
        send_ref[block, :, width:] = extra_ref[block]
    scale_ref[...] = jnp.broadcast_to(scale, scale_ref.shape)
    normed = (xhat * gain_ref[...] + shift_ref[...]).astype(BF16)
    tables = (cos_ref[...], up_ref[...], down_ref[...])
    query = kernel_turn(dot(normed, w_ref[:, :width]) + bq_ref[...], tables, 1.0)
    key = kernel_turn(dot(normed, w_ref[:, width : 2 * width]), tables, 1.0)
    value = dot(normed, w_ref[:, 2 * width :]) + bv_ref[...]
    seqs = rows // (2 * BLK)
    for s in range(seqs):
        at = s * 2 * BLK
        whole, early, late = slice(at, at + 2 * BLK), slice(at, at + BLK), slice(at + BLK, at + 2 * BLK)
        for h in range(HEADS):
            pair = jnp.concatenate([head(query, whole, h), head(key, whole, h)], axis=1)
            out_ref[s * HEADS + h, : 2 * BLK, :] = pair.astype(BF16)
            pair = jnp.concatenate([head(value, early, h), head(value, late, h)], axis=1)
            out_ref[s * HEADS + h, 2 * BLK :, :] = pair.astype(BF16)
    spare = out_ref.shape[0] - seqs * HEADS
    out_ref[seqs * HEADS :, :, :] = jnp.zeros((spare,) + out_ref.shape[1:], BF16)


def on_chip(kernel, out_shape, name, flops, *operands, scratch=()):
    many = isinstance(out_shape, tuple)
    spec = pl.BlockSpec(memory_space=pltpu.VMEM)
    return pl.pallas_call(
        kernel,
        out_shape=out_shape,
        in_specs=[spec] * len(operands),
        out_specs=[spec] * len(out_shape) if many else spec,
        scratch_shapes=list(scratch),
        compiler_params=pltpu.CompilerParams(vmem_limit_bytes=48 << 20),
        cost_estimate=pl.CostEstimate(flops=flops, bytes_accessed=8_000_000, transcendentals=0),
        name=name,
    )(*operands)


def shaped(shape, dtype):
    return jax.ShapeDtypeStruct(shape, dtype)


def mix(x, w, tables, extra):
    rows, width = x.shape
    count = lax.axis_size("ctx")
    shapes = (
        shaped((rows, width), F32),
        shaped((extra.shape[0], rows, width + extra.shape[2]), BF16),
        shaped((rows, 128), F32),
        shaped((count, 3 * BLK, 128), BF16),
    )
    return on_chip(mix_kernel, shapes, "mix", 5_000_000_000, x, w["g_attn"], w["s_attn"], w["qkv"], w["b_q"], w["b_v"], *tables, extra)


def join_kernel(tile_ref, x_ref, mlp_ref, w_ref, bias_ref, split_ref, out_ref, context):
    rows, width = context.shape
    for s in range(rows // (2 * BLK)):
        for half in range(2):
            at = (2 * s + half) * BLK
            lanes = slice(half * HEAD_DIM, (half + 1) * HEAD_DIM)
            row = [tile_ref[s * HEADS + h, :, lanes] for h in range(HEADS)]
            context[at : at + BLK, :] = jnp.concatenate(row, axis=1)
    size = width // 4
    for block in range(4):
        split_ref[block] = context[:, block * size : (block + 1) * size]
    out_ref[...] = x_ref[...] + dot(context[...], w_ref[...]) + (mlp_ref[...] + bias_ref[...])


def join(tiles, x, mlp, w):
    rows, width = x.shape
    shapes = (shaped((4, rows, width // 4), BF16), shaped((rows, width), F32))
    scratch = [pltpu.VMEM((rows, width), BF16)]
    return on_chip(join_kernel, shapes, "join", 500_000_000, tiles, x, mlp, w["out"], w["b_out"] + w["b_down"], scratch=scratch)


def pull_kernel(g_ref, w_ref, out_ref):
    grad = dot(g_ref[...], w_ref[...], NT)
    seqs = grad.shape[0] // (2 * BLK)
    for s in range(seqs):
        at = s * 2 * BLK
        for h in range(HEADS):
            early, late = head(grad, slice(at, at + BLK), h), head(grad, slice(at + BLK, at + 2 * BLK), h)
            out_ref[s * HEADS + h] = jnp.concatenate([early, late], axis=1).astype(BF16)
    spare = out_ref.shape[0] - seqs * HEADS
    out_ref[seqs * HEADS :, :, :] = jnp.zeros((spare,) + out_ref.shape[1:], BF16)


def pull(g_low, w):
    count = lax.axis_size("ctx")
    return on_chip(pull_kernel, shaped((count, BLK, 128), BF16), "pull", 500_000_000, g_low, w["out"])


def unmix_kernel(tile_ref, cos_ref, up_ref, down_ref, mixed_ref, split_ref, sums_ref):
    rows, width = cos_ref.shape
    tables = (cos_ref[...], up_ref[...], down_ref[...])
    parts = [[], [], []]
    for s in range(rows // (2 * BLK)):
        for part in range(2):
            lanes = slice(part * HEAD_DIM, (part + 1) * HEAD_DIM)
            row = [tile_ref[s * HEADS + h, : 2 * BLK, lanes] for h in range(HEADS)]
            parts[part].append(jnp.concatenate(row, axis=1))
        for half in range(2):
            lanes = slice(half * HEAD_DIM, (half + 1) * HEAD_DIM)
            row = [tile_ref[s * HEADS + h, 2 * BLK : 3 * BLK, lanes] for h in range(HEADS)]
            parts[2].append(jnp.concatenate(row, axis=1))
    query, key, value = (jnp.concatenate(part, axis=0) for part in parts)
    mixed_ref[:, :width] = kernel_turn(query.astype(F32), tables, -1.0).astype(BF16)
    mixed_ref[:, width : 2 * width] = kernel_turn(key.astype(F32), tables, -1.0).astype(BF16)
    mixed_ref[:, 2 * width :] = value
    size = 3 * width // 4
    for block in range(4):
        split_ref[block] = mixed_ref[:, block * size : (block + 1) * size]
    sums_ref[...] = jnp.sum(mixed_ref[...].astype(F32), axis=0, keepdims=True)


def unmix(tiles, tables):
    rows, width = tables[0].shape
    shapes = (
        shaped((rows, 3 * width), BF16),
        shaped((4, rows, 3 * width // 4), BF16),
        shaped((1, 3 * width), F32),
    )
    return on_chip(unmix_kernel, shapes, "unmix", 500_000_000, tiles, *tables)


def norm_kernel(mixed_ref, w_ref, g_ref, mlp_ref, xhat_ref, scale_ref, ga_ref, gm_ref, split_ref, context_ref, out_ref, low_ref, send_ref, sums_ref):
    attn = dot(mixed_ref[...], w_ref[...], NT)
    mlp, xhat, g = mlp_ref[...], xhat_ref[...], g_ref[...]
    both = attn * ga_ref[...] + mlp * gm_ref[...]
    inner = both - jnp.mean(both, axis=-1, keepdims=True) - xhat * jnp.mean(both * xhat, axis=-1, keepdims=True)
    new = g + scale_ref[:, :1] * inner
    out_ref[...] = new
    low_ref[...] = new.astype(BF16)
    if send_ref.shape[0] == 4:
        width = new.shape[1]
        size, rest = split_ref.shape[2], context_ref.shape[2]
        send_ref[...] = jnp.zeros_like(send_ref)
        for block in range(4):
            send_ref[block, :, :width] = new.astype(BF16)
            send_ref[block, :, width : width + size] = split_ref[block]
            send_ref[block, :, send_ref.shape[2] - rest :] = context_ref[block]
    sums_ref[...] = jnp.zeros_like(sums_ref)
    for row, value in enumerate((attn * xhat, attn, mlp * xhat, mlp, g.astype(BF16).astype(F32))):
        sums_ref[row : row + 1, :] = jnp.sum(value, axis=0, keepdims=True)


def norm_backward(g, mixed, grad_n_mlp, xhat, scale, w, split, context, send):
    rows, width = g.shape
    size = -(-split.shape[2] // 128) * 128
    sent = (4, rows, width + size + context.shape[2]) if send else (1, 8, 128)
    shapes = (shaped((rows, width), F32), shaped((rows, width), BF16), shaped(sent, BF16), shaped((8, width), F32))
    return on_chip(
        norm_kernel, shapes, "norm_back", 1_500_000_000, mixed, w["qkv"], g, grad_n_mlp, xhat, scale, w["g_attn"], w["g_mlp"], split, context
    )


def rotary_tables(seqs):
    device = lax.axis_index("ctx")
    devices = lax.axis_size("ctx")
    offsets = jnp.arange(BLK, dtype=jnp.int32)
    early = device * BLK + offsets
    late = 2 * BLK * devices - (device + 1) * BLK + offsets
    positions = jnp.tile(jnp.concatenate([early, late]), seqs).astype(F32)
    half = ROT // 2
    frequency = 10000.0 ** (-jnp.arange(half, dtype=F32) * 2.0 / ROT)
    angles = positions[:, None] * frequency[None, :]
    cosine, sine = lax.optimization_barrier((jnp.cos(angles), jnp.sin(angles)))
    rows = positions.shape[0]
    zero = jnp.zeros((rows, half), F32)
    rest = HEAD_DIM - ROT

    def whole(first, second, fill):
        return jnp.tile(jnp.concatenate([first, second, jnp.full((rows, rest), fill, F32)], axis=1), (1, HEADS))

    tables = (whole(cosine, cosine, 1.0), whole(zero, sine, 0.0), whole(sine, zero, 0.0))
    return lax.optimization_barrier(tables)


def cdf(value):
    return 0.5 * (1.0 + lax.erf(value * (0.5 ** 0.5)))


TN = (((0,), (0,)), ((), ()))


def split_columns(value):
    return value.reshape(value.shape[0], 4, -1).transpose(1, 0, 2)


def mlp_forward(xhat_all, w):
    n_mlp_all = (xhat_all.astype(F32) * w["g_mlp"] + w["s_mlp"]).astype(BF16)
    hidden = dot(n_mlp_all, w["up"]) + w["b_up"]
    active = (hidden * cdf(hidden)).astype(BF16)
    return n_mlp_all, hidden, active, dot(active, w["down"])


def own_sum(partial):
    rows = partial.shape[0] // 4
    return group_sum([partial[i * rows : (i + 1) * rows] for i in range(4)])


def mlp_backward(g_all, n_mlp_all, hidden, active, w):
    grad_active = dot(g_all, w["down"], NT)
    density = jnp.exp(-0.5 * hidden * hidden) * 0.3989422804014327
    grad_hidden = (grad_active * (cdf(hidden) + hidden * density)).astype(BF16)
    partial = dot(grad_hidden, w["up"], NT)
    grad_down = dot(active, g_all, TN).astype(BF16)
    grad_up = dot(n_mlp_all, grad_hidden, TN).astype(BF16)
    grad_b_up = jnp.sum(grad_hidden.astype(F32), axis=0)
    return partial, grad_down, grad_up.reshape(4, -1, grad_up.shape[1]), grad_b_up


def small_sums(sums, mixed_sums):
    width = sums.shape[1]
    bias = jnp.concatenate([mixed_sums[0, :width], mixed_sums[0, 2 * width :]])
    rest = sums[:5].reshape(5, 4, -1).transpose(1, 0, 2).reshape(4, -1)
    return jnp.concatenate([rest, bias.reshape(4, -1)], axis=1)


def gather_small(stacked):
    names = ("g_attn", "s_attn", "g_mlp", "s_mlp", "b_qv", "b_out", "b_down")
    flat = jnp.concatenate([stacked[name] for name in names], axis=1)
    every = spread(flat, "wt").astype(F32)
    found, at = {}, 0
    for name in names:
        size = stacked[name].shape[1]
        found[name] = every[:, :, at : at + size].transpose(1, 0, 2).reshape(LAYERS, -1)
        at += size
    return found


def local(tokens_in, cotangent, ln_gain_attn, ln_shift_attn, ln_gain_mlp, ln_shift_mlp, w_qkv, b_qv, w_out, b_out, w_up, b_up, w_down, b_down):
    seqs = tokens_in.shape[0]
    width = tokens_in.shape[3]
    rows = seqs * 2 * BLK
    devices = lax.axis_size("ctx")
    depth = width // 4
    unit = b_up.shape[1]
    tables = rotary_tables(seqs)
    small = gather_small(
        {"g_attn": ln_gain_attn, "s_attn": ln_shift_attn, "g_mlp": ln_gain_mlp, "s_mlp": ln_shift_mlp, "b_qv": b_qv, "b_out": b_out, "b_down": b_down}
    )
    half1 = gather_half(w_qkv[0])
    qkv = [gather_rest(half1), lax.all_gather(w_qkv[1], "wt", axis=0, tiled=True)]
    out_both = lax.all_gather(w_out, "wt", axis=1, tiled=True)
    layers = []
    for layer in range(LAYERS):
        w = {name: small[name][layer][None] for name in small}
        w["b_q"] = w["b_qv"][:, :width]
        w["b_v"] = w["b_qv"][:, width:]
        w["qkv"] = qkv[layer]
        w["out"] = out_both[layer]
        w["down"] = w_down[layer]
        w["b_up"] = b_up[layer].astype(F32)[None]
        layers.append(w)
    first, second = layers
    g2 = cotangent.reshape(rows, width)
    x1 = tokens_in.reshape(rows, width).astype(F32)
    xhat1, send1, scale1, packed1 = mix(x1, first, tables, jnp.zeros((1, rows, 128), BF16))
    later_up, send1 = after((w_up, send1), packed1)
    packed1 = exchange(packed1, "ctx")
    ups = jnp.stack([later_up[:, :, i * unit : (i + 1) * unit] for i in range(4)])
    ups = group_trade(ups)
    spread1 = group_spread(send1[0, :, :width])
    out1, full1, lse1 = attend(packed1)
    both1 = jnp.concatenate([out1, pull(g2, second)], axis=1)
    ups, spread1, later_g2 = after((ups, spread1, g2), both1)
    both1 = exchange(both1, "ctx")
    ups = place([b[:, None] for b in ups], 1).reshape(LAYERS, width, unit)
    first["up"], second["up"] = ups[0], ups[1]
    xhat1_all = jnp.concatenate(spread1, axis=0)
    n_mlp1, hidden1, active1, partial1 = mlp_forward(xhat1_all, first)
    mlp1 = own_sum(partial1)
    out1, grads2 = both1[:, :BLK], both1[:, BLK:]
    split1, x2 = join(out1, x1, mlp1, first)
    xhat2, send2, scale2, packed2 = mix(x2, second, tables, split1)
    packed2 = exchange(packed2, "ctx")
    g2_all = jnp.concatenate(group_spread(after(later_g2, mlp1)), axis=0)
    landed2 = jnp.concatenate(group_trade(send2), axis=0)
    xhat2_all, context1_all = landed2[:, :width], landed2[:, width:]
    n_mlp2, hidden2, active2, partial2 = mlp_forward(xhat2_all, second)
    out2, full2, lse2 = attend(packed2)
    back2 = exchange(attend_back(packed2, grads2, full2, lse2, out2), "ctx")
    back_partial2, grad_down2, grad_up2, grad_b_up2 = mlp_backward(g2_all, n_mlp2, hidden2, active2, second)
    sums = own_sum(jnp.concatenate([partial2, back_partial2], axis=1))
    mlp2, grad_n_mlp2 = sums[:, :width], sums[:, width:]
    split2, x3 = join(back2[:, 3 * BLK :], x2, mlp2, second)
    out_tokens = x3.astype(BF16).reshape(tokens_in.shape)
    mixed2, mixed2_split, mixed_sums2 = unmix(back2, tables)
    g1, g1_low, send3, sums2 = norm_backward(g2.astype(F32), mixed2, grad_n_mlp2, xhat2, scale2, second, mixed2_split, split2, True)
    grads1 = exchange(pull(g1_low, first), "ctx")
    landed3 = jnp.concatenate(group_trade(send3), axis=0)
    columns = mixed2_split.shape[2]
    g1_all, mixed2_all, context2_all = landed3[:, :width], landed3[:, width : width + columns], landed3[:, -depth:]
    back_partial1, grad_down1, grad_up1, grad_b_up1 = mlp_backward(g1_all, n_mlp1, hidden1, active1, first)
    back1 = exchange(attend_back(packed1, grads1, full1, lse1, lse1[None].astype(BF16)), "ctx")
    grad_up1 = place([b[None] for b in group_trade(grad_up1)], 0).reshape(width, unit)
    grad_out1 = dot(context1_all, g1_all, TN).astype(BF16)
    grad_out2 = dot(context2_all, g2_all, TN).astype(BF16)
    n_attn2_all = (xhat2_all.astype(F32) * second["g_attn"] + second["s_attn"]).astype(BF16)
    grad_up2 = place([b[None] for b in group_trade(grad_up2)], 0).reshape(width, unit)
    ready = [grad_down1, grad_up1, grad_down2, grad_up2, grad_out1, grad_out2]
    lines = sum(v.shape[0] for v in ready)
    lines = -(-lines // (16 * devices)) * 16 * devices - lines
    ready = jnp.concatenate(ready + [jnp.zeros((lines, width), BF16)], axis=0)
    back1, ready = lax.optimization_barrier((back1, ready))
    wide = lax.psum_scatter(ready, "ctx", scatter_dimension=0, tiled=True)
    mixed1, mixed1_split, mixed_sums1 = unmix(back1, tables)
    mixed1_all = jnp.concatenate(group_trade(mixed1_split), axis=0)
    back_partial1, mixed2_all = after((back_partial1, mixed2_all), mixed1_split)
    grad_n_mlp1 = own_sum(back_partial1)
    grad_qkv2 = dot(n_attn2_all, mixed2_all, TN).astype(BF16)
    n_attn1_all = (xhat1_all.astype(F32) * first["g_attn"] + first["s_attn"]).astype(BF16)
    grad_qkv1 = dot(n_attn1_all, mixed1_all, TN).astype(BF16)
    g0, _, _, sums1 = norm_backward(g1, mixed1, grad_n_mlp1, xhat1, scale1, first, mixed2_split, split2, False)
    small1, small2 = small_sums(sums1, mixed_sums1), small_sums(sums2, mixed_sums2)
    smalls, hidden_sums = (small1, small2), (grad_b_up1, grad_b_up2)
    piece = width // devices

    def to_rows(value):
        size = value.shape[-1]
        lines = -(-size // columns)
        lines = -(-lines // 8) * 8
        padded = jnp.pad(value, ((0, 0), (0, lines * columns - size)))
        return padded.reshape(value.shape[0], lines, columns)

    tiny = to_rows(jnp.concatenate(smalls, axis=1).astype(BF16))
    both_qkv = [m.reshape(4, depth, columns) for m in (grad_qkv1, grad_qkv2)]
    moved = exchange(jnp.concatenate(both_qkv + [tiny], axis=1), "wt")
    tiny_size = small1.shape[1]
    small_sum = moved[:, 2 * depth :].astype(F32).sum(0).reshape(1, -1)[:, : LAYERS * tiny_size]
    tail = to_rows(jnp.concatenate([small_sum, *(u[None] for u in hidden_sums)], axis=1).astype(BF16))
    sent = jnp.concatenate(
        [moved[:, i * depth : (i + 1) * depth].reshape(devices, piece, columns) for i in range(LAYERS)]
        + [jnp.broadcast_to(tail, (devices,) + tail.shape[1:])],
        axis=1,
    )
    landed = exchange(sent, "ctx").astype(F32).sum(0)
    def side_by_side(blocks):
        return blocks.transpose(1, 0, 2).reshape(depth, -1)

    qkvs = spread(landed[: 2 * piece].astype(BF16), "ctx")
    wide = lax.all_gather(after(wide, landed), "ctx", axis=0, tiled=True)
    at = 2 * (unit + width)
    down1, up1 = wide[:unit], wide[unit : unit + width].reshape(4, depth, unit)
    down2, up2 = wide[unit + width : 2 * unit + width], wide[2 * unit + width : at].reshape(4, depth, unit)
    qkvs = [side_by_side(qkvs[:, i * piece : (i + 1) * piece].reshape(4, depth, columns)) for i in range(LAYERS)]
    flat = landed[2 * piece :].reshape(-1)
    per_layer = [flat[layer * tiny_size : (layer + 1) * tiny_size] for layer in range(LAYERS)]
    grad_b_up = flat[LAYERS * tiny_size :][: LAYERS * unit].reshape(LAYERS, unit)

    def vector(index):
        return jnp.stack([v[index * depth : (index + 1) * depth] for v in per_layer])

    def both(one, two):
        return jnp.stack([one.astype(F32), two.astype(F32)])

    grad_bias = vector(4)
    grad_b_qv = jnp.stack([v[5 * depth :] for v in per_layer])
    grad_qkv = both(*qkvs)
    return (
        out_tokens,
        g0.reshape(tokens_in.shape),
        vector(0),
        vector(1),
        vector(2),
        vector(3),
        grad_qkv,
        grad_b_qv,
        both(wide[at : at + depth], wide[at + depth : at + 2 * depth]),
        grad_bias,
        both(side_by_side(up1), side_by_side(up2)),
        grad_b_up,
        both(down1, down2),
        grad_bias,
    )


def solution(mesh):
    tokens = P("wt", None, "ctx", None)
    vec, mat = P(None, "wt"), P(None, "wt", None)
    params = (vec, vec, vec, vec, mat, vec, mat, vec, mat, vec, mat, vec)
    return jax.shard_map(
        local,
        mesh=mesh,
        in_specs=(tokens, tokens) + params,
        out_specs=(tokens, tokens) + params,
        check_vma=False,
    )
```

```python
from functools import partial

import jax
import jax.numpy as jnp
from jax import lax
from jax.experimental import pallas as pl
from jax.experimental.pallas import tpu as pltpu
from jax.sharding import PartitionSpec as P

HEADS = 12
HEAD_DIM = 64
ROT = 16
LAYERS = 2
BLK = 32
EPS = 1e-05

F32 = jnp.float32
BF16 = jnp.bfloat16
NT = (((1,), (1,)), ((), ()))
NN = (((1,), (0,)), ((), ()))
TILE = 512


def dot(left, right, dims=NN):
    return lax.dot_general(left, right, dims, preferred_element_type=F32)


def exchange(chunks, axis):
    return lax.all_to_all(chunks, axis, 0, 0, tiled=True)


def pass_on(value, shift):
    count = lax.axis_size("wt")
    return lax.ppermute(value, "wt", [(i, (i + shift) % count) for i in range(count)])


def shifts():
    return (1, 3, 2)


def group_spread(value):
    landed = {0: value}
    for shift in shifts():
        landed[shift] = pass_on(value, shift)
    return [landed[shift] for shift in range(4)]


def group_sum(blocks):
    total = blocks[0]
    for shift in shifts():
        total = total + pass_on(blocks[shift].astype(BF16), (4 - shift) % 4).astype(F32)
    return total


def group_trade(chunks):
    here = lax.axis_index("wt")

    def chunk(shift):
        return lax.dynamic_index_in_dim(chunks, (here + shift) % 4, 0, keepdims=False)

    landed = {0: chunk(0)}
    for shift in shifts():
        landed[shift] = pass_on(chunk(shift), shift)
    return [landed[shift] for shift in range(4)]


def place(blocks, axis):
    here = lax.axis_index("wt")
    shape = list(blocks[0].shape)
    size = shape[axis]
    shape[axis] = 4 * size
    whole = jnp.zeros(shape, blocks[0].dtype)
    for shift in range(4):
        whole = lax.dynamic_update_slice_in_dim(whole, blocks[shift], ((here - shift) % 4) * size, axis)
    return whole


def swap(value):
    return lax.ppermute(value, "ctx", [(i, i ^ 1) for i in range(lax.axis_size("ctx"))])


def gather_half(shard):
    core = lax.axis_index("ctx") % 2
    half = shard.shape[0] // 2
    mine = lax.dynamic_slice_in_dim(shard, core * half, half, 0)
    return place([b[None] for b in group_spread(mine)], 0)


def gather_rest(here):
    core = lax.axis_index("ctx") % 2
    other = swap(here)
    first = jnp.where(core == 0, here, other)
    second = jnp.where(core == 0, other, here)
    return jnp.stack([first, second], axis=1).reshape(-1, here.shape[2])


def after(values, first):
    return lax.optimization_barrier((values, first))[0]


def spread(value, axis):
    count = lax.axis_size(axis)
    return exchange(jnp.broadcast_to(value[None], (count,) + value.shape), axis)


def tile_list(size):
    tiles = []
    for start in range(0, size, TILE):
        keys = [(0, k, k == start) for k in range(0, start + TILE, TILE)]
        tiles.append((0, start, keys))
    for start in range(0, size, TILE):
        keys = [(0, k, False) for k in range(0, size, TILE)]
        keys += [(1, k, k == start) for k in range(start, size, TILE)]
        tiles.append((1, start, keys))
    return tiles


def tile_mask(half):
    row = lax.broadcasted_iota(jnp.int32, (TILE, TILE), 0)
    col = lax.broadcasted_iota(jnp.int32, (TILE, TILE), 1)
    if half:
        shift = BLK.bit_length() - 1
        row_pos = (row & (BLK - 1)) - ((row >> shift) << shift)
        col_pos = (col & (BLK - 1)) - ((col >> shift) << shift)
        return row_pos <= col_pos
    return row <= col


def forward_kernel(in_ref, out_ref, full_ref, lse_ref, q_scr, k_scr, vt_scr):
    count = in_ref.shape[0]
    size = count * BLK
    for half in range(2):
        both = in_ref[:, half * BLK : (half + 1) * BLK, :].reshape(size, 128)
        q_scr[half] = both[:, :64] * jnp.asarray(HEAD_DIM ** -0.5, BF16)
        k_scr[half] = both[:, 64:]
    values = in_ref[:, 2 * BLK : 3 * BLK, :].reshape(size, 128)
    vt_scr[...] = values.astype(F32).T.astype(BF16)
    for half, start, keys in tile_list(size):
        query = q_scr[half, start : start + TILE, :]
        top = jnp.full((1, TILE), -1e30, F32)
        total = jnp.zeros((1, TILE), F32)
        acc = jnp.zeros((64, TILE), F32)
        for key_half, key_start, masked in keys:
            key = k_scr[key_half, key_start : key_start + TILE, :]
            scores = dot(key, query, NT)
            if masked:
                scores = jnp.where(tile_mask(half), scores, -1e30)
            new_top = jnp.maximum(top, jnp.max(scores, axis=0, keepdims=True))
            raised = jnp.exp(scores - new_top)
            keep = jnp.exp(top - new_top)
            total = total * keep + jnp.sum(raised, axis=0, keepdims=True)
            value = vt_scr[key_half * 64 : (key_half + 1) * 64, key_start : key_start + TILE]
            acc = acc * keep + dot(value, raised.astype(BF16))
            top = new_top
        full_ref[half * 64 : (half + 1) * 64, start : start + TILE] = acc / total
        lse_ref[half : half + 1, start : start + TILE] = top + jnp.log(total)
    out_ref[...] = full_ref[...].T.astype(BF16).reshape(count, BLK, 128)


def backward_kernel(in_ref, grad_ref, full_ref, lse_ref, carry_ref, out_ref, q_scr, k_scr, kt_scr, v_scr, do_scr, delta_scr, dq_scr, dk_scr, dv_scr):
    count = in_ref.shape[0]
    size = count * BLK
    grads = grad_ref[...].reshape(size, 128)
    grads_t = grads.astype(F32).T
    product = grads_t * full_ref[...]
    values = in_ref[:, 2 * BLK : 3 * BLK, :].reshape(size, 128)
    for half in range(2):
        both = in_ref[:, half * BLK : (half + 1) * BLK, :].reshape(size, 128)
        q_scr[half] = both[:, :64] * jnp.asarray(HEAD_DIM ** -0.5, BF16)
        k_scr[half] = both[:, 64:]
        kt_scr[half] = both.astype(F32).T[64:, :].astype(BF16)
        lanes = slice(half * 64, (half + 1) * 64)
        v_scr[half] = values[:, lanes]
        do_scr[half] = grads[:, lanes]
        delta_scr[half : half + 1, :] = jnp.sum(product[lanes, :], axis=0, keepdims=True)
    dk_scr[...] = jnp.zeros_like(dk_scr)
    dv_scr[...] = jnp.zeros_like(dv_scr)
    for half, start, keys in tile_list(size):
        rows = slice(start, start + TILE)
        query = q_scr[half, rows, :]
        grad = do_scr[half, rows, :]
        lse = lse_ref[half : half + 1, rows]
        delta = delta_scr[half : half + 1, rows]
        acc = jnp.zeros((64, TILE), F32)
        for key_half, key_start, masked in keys:
            key_rows = slice(key_start, key_start + TILE)
            scores = dot(k_scr[key_half, key_rows, :], query, NT)
            if masked:
                scores = jnp.where(tile_mask(half), scores, -1e30)
            probs = jnp.exp(scores - lse)
            grad_probs = dot(v_scr[key_half, key_rows, :], grad, NT)
            grad_scores = (probs * (grad_probs - delta)).astype(BF16)
            dv_scr[key_half, key_rows, :] += dot(probs.astype(BF16), grad)
            dk_scr[key_half, key_rows, :] += dot(grad_scores, query)
            acc += dot(kt_scr[key_half, :, key_rows], grad_scores)
        dq_scr[half * 64 : (half + 1) * 64, rows] = acc * (HEAD_DIM ** -0.5)
    queries = dq_scr[...].T
    for half in range(2):
        both = jnp.concatenate([queries[:, half * 64 : (half + 1) * 64], dk_scr[half]], axis=1)
        out_ref[:, half * BLK : (half + 1) * BLK, :] = both.astype(BF16).reshape(count, BLK, 128)
    if carry_ref.shape[1] > 8:
        out_ref[:, 3 * BLK :, :] = carry_ref[...]
    both = jnp.concatenate([dv_scr[0], dv_scr[1]], axis=1)
    out_ref[:, 2 * BLK : 3 * BLK, :] = both.astype(BF16).reshape(count, BLK, 128)


def attend(packed):
    count = packed.shape[0]
    size = count * BLK
    return pl.pallas_call(
        forward_kernel,
        out_shape=(
            jax.ShapeDtypeStruct((count, BLK, 128), BF16),
            jax.ShapeDtypeStruct((128, size), F32),
            jax.ShapeDtypeStruct((8, size), F32),
        ),
        in_specs=[pl.BlockSpec(memory_space=pltpu.VMEM)],
        out_specs=[pl.BlockSpec(memory_space=pltpu.VMEM)] * 3,
        scratch_shapes=[
            pltpu.VMEM((2, size, 64), BF16),
            pltpu.VMEM((2, size, 64), BF16),
            pltpu.VMEM((128, size), BF16),
        ],
        compiler_params=pltpu.CompilerParams(vmem_limit_bytes=48 << 20),
        cost_estimate=pl.CostEstimate(flops=20_000_000_000, bytes_accessed=20_000_000, transcendentals=2_600_000),
        name="attend",
    )(packed)


def attend_back(packed, grads, full, lse, carry):
    extra = carry.shape[1] if carry.shape[1] > 8 else 0
    count = packed.shape[0]
    size = count * BLK
    return pl.pallas_call(
        backward_kernel,
        out_shape=jax.ShapeDtypeStruct((count, 3 * BLK + extra, 128), BF16),
        in_specs=[pl.BlockSpec(memory_space=pltpu.VMEM)] * 5,
        out_specs=pl.BlockSpec(memory_space=pltpu.VMEM),
        scratch_shapes=[
            pltpu.VMEM((2, size, 64), BF16),
            pltpu.VMEM((2, size, 64), BF16),
            pltpu.VMEM((2, 64, size), BF16),
            pltpu.VMEM((2, size, 64), BF16),
            pltpu.VMEM((2, size, 64), BF16),
            pltpu.VMEM((8, size), F32),
            pltpu.VMEM((128, size), F32),
            pltpu.VMEM((2, size, 64), F32),
            pltpu.VMEM((2, size, 64), F32),
        ],
        compiler_params=pltpu.CompilerParams(vmem_limit_bytes=48 << 20),
        cost_estimate=pl.CostEstimate(flops=40_000_000_000, bytes_accessed=40_000_000, transcendentals=2_600_000),
        name="attend_back",
    )(packed, grads, full, lse, carry)


def kernel_turn(value, tables, sign):
    cosine, up, down = tables
    half = ROT // 2
    back = value.shape[1] - half
    turned = pltpu.roll(value, half, 1) * up - pltpu.roll(value, back, 1) * down
    return value * cosine + sign * turned


def head(value, rows, index):
    return value[rows, index * HEAD_DIM : (index + 1) * HEAD_DIM]


def mix_kernel(x_ref, gain_ref, shift_ref, w_ref, bq_ref, bv_ref, cos_ref, up_ref, down_ref, extra_ref, xhat_ref, send_ref, scale_ref, out_ref):
    x = x_ref[...]
    rows, width = x.shape
    centred = x - jnp.mean(x, axis=-1, keepdims=True)
    scale = lax.rsqrt(jnp.mean(centred * centred, axis=-1, keepdims=True) + EPS)
    xhat = centred * scale
    xhat_ref[...] = xhat
    for block in range(send_ref.shape[0]):
        send_ref[block, :, :width] = xhat.astype(BF16)
        send_ref[block, :, width:] = extra_ref[block]
    scale_ref[...] = jnp.broadcast_to(scale, scale_ref.shape)
    normed = (xhat * gain_ref[...] + shift_ref[...]).astype(BF16)
    tables = (cos_ref[...], up_ref[...], down_ref[...])
    query = kernel_turn(dot(normed, w_ref[:, :width]) + bq_ref[...], tables, 1.0)
    key = kernel_turn(dot(normed, w_ref[:, width : 2 * width]), tables, 1.0)
    value = dot(normed, w_ref[:, 2 * width :]) + bv_ref[...]
    seqs = rows // (2 * BLK)
    for s in range(seqs):
        at = s * 2 * BLK
        whole, early, late = slice(at, at + 2 * BLK), slice(at, at + BLK), slice(at + BLK, at + 2 * BLK)
        for h in range(HEADS):
            pair = jnp.concatenate([head(query, whole, h), head(key, whole, h)], axis=1)
            out_ref[s * HEADS + h, : 2 * BLK, :] = pair.astype(BF16)
            pair = jnp.concatenate([head(value, early, h), head(value, late, h)], axis=1)
            out_ref[s * HEADS + h, 2 * BLK :, :] = pair.astype(BF16)
    spare = out_ref.shape[0] - seqs * HEADS
    out_ref[seqs * HEADS :, :, :] = jnp.zeros((spare,) + out_ref.shape[1:], BF16)


def on_chip(kernel, out_shape, name, flops, *operands, scratch=()):
    many = isinstance(out_shape, tuple)
    spec = pl.BlockSpec(memory_space=pltpu.VMEM)
    return pl.pallas_call(
        kernel,
        out_shape=out_shape,
        in_specs=[spec] * len(operands),
        out_specs=[spec] * len(out_shape) if many else spec,
        scratch_shapes=list(scratch),
        compiler_params=pltpu.CompilerParams(vmem_limit_bytes=48 << 20),
        cost_estimate=pl.CostEstimate(flops=flops, bytes_accessed=8_000_000, transcendentals=0),
        name=name,
    )(*operands)


def shaped(shape, dtype):
    return jax.ShapeDtypeStruct(shape, dtype)


def mix(x, w, tables, extra):
    rows, width = x.shape
    count = lax.axis_size("ctx")
    shapes = (
        shaped((rows, width), F32),
        shaped((extra.shape[0], rows, width + extra.shape[2]), BF16),
        shaped((rows, 128), F32),
        shaped((count, 3 * BLK, 128), BF16),
    )
    return on_chip(mix_kernel, shapes, "mix", 5_000_000_000, x, w["g_attn"], w["s_attn"], w["qkv"], w["b_q"], w["b_v"], *tables, extra)


def join_kernel(tile_ref, x_ref, mlp_ref, w_ref, bias_ref, split_ref, out_ref, context):
    rows, width = context.shape
    for s in range(rows // (2 * BLK)):
        for half in range(2):
            at = (2 * s + half) * BLK
            lanes = slice(half * HEAD_DIM, (half + 1) * HEAD_DIM)
            row = [tile_ref[s * HEADS + h, :, lanes] for h in range(HEADS)]
            context[at : at + BLK, :] = jnp.concatenate(row, axis=1)
    size = width // 4
    for block in range(4):
        split_ref[block] = context[:, block * size : (block + 1) * size]
    out_ref[...] = x_ref[...] + dot(context[...], w_ref[...]) + (mlp_ref[...] + bias_ref[...])


def join(tiles, x, mlp, w):
    rows, width = x.shape
    shapes = (shaped((4, rows, width // 4), BF16), shaped((rows, width), F32))
    scratch = [pltpu.VMEM((rows, width), BF16)]
    return on_chip(join_kernel, shapes, "join", 500_000_000, tiles, x, mlp, w["out"], w["b_out"] + w["b_down"], scratch=scratch)


def pull_kernel(g_ref, w_ref, out_ref):
    grad = dot(g_ref[...], w_ref[...], NT)
    seqs = grad.shape[0] // (2 * BLK)
    for s in range(seqs):
        at = s * 2 * BLK
        for h in range(HEADS):
            early, late = head(grad, slice(at, at + BLK), h), head(grad, slice(at + BLK, at + 2 * BLK), h)
            out_ref[s * HEADS + h] = jnp.concatenate([early, late], axis=1).astype(BF16)
    spare = out_ref.shape[0] - seqs * HEADS
    out_ref[seqs * HEADS :, :, :] = jnp.zeros((spare,) + out_ref.shape[1:], BF16)


def pull(g_low, w):
    count = lax.axis_size("ctx")
    return on_chip(pull_kernel, shaped((count, BLK, 128), BF16), "pull", 500_000_000, g_low, w["out"])


def unmix_kernel(tile_ref, cos_ref, up_ref, down_ref, mixed_ref, split_ref, sums_ref):
    rows, width = cos_ref.shape
    tables = (cos_ref[...], up_ref[...], down_ref[...])
    parts = [[], [], []]
    for s in range(rows // (2 * BLK)):
        for part in range(2):
            lanes = slice(part * HEAD_DIM, (part + 1) * HEAD_DIM)
            row = [tile_ref[s * HEADS + h, : 2 * BLK, lanes] for h in range(HEADS)]
            parts[part].append(jnp.concatenate(row, axis=1))
        for half in range(2):
            lanes = slice(half * HEAD_DIM, (half + 1) * HEAD_DIM)
            row = [tile_ref[s * HEADS + h, 2 * BLK : 3 * BLK, lanes] for h in range(HEADS)]
            parts[2].append(jnp.concatenate(row, axis=1))
    query, key, value = (jnp.concatenate(part, axis=0) for part in parts)
    mixed_ref[:, :width] = kernel_turn(query.astype(F32), tables, -1.0).astype(BF16)
    mixed_ref[:, width : 2 * width] = kernel_turn(key.astype(F32), tables, -1.0).astype(BF16)
    mixed_ref[:, 2 * width :] = value
    size = 3 * width // 4
    for block in range(4):
        split_ref[block] = mixed_ref[:, block * size : (block + 1) * size]
    sums_ref[...] = jnp.sum(mixed_ref[...].astype(F32), axis=0, keepdims=True)


def unmix(tiles, tables):
    rows, width = tables[0].shape
    shapes = (
        shaped((rows, 3 * width), BF16),
        shaped((4, rows, 3 * width // 4), BF16),
        shaped((1, 3 * width), F32),
    )
    return on_chip(unmix_kernel, shapes, "unmix", 500_000_000, tiles, *tables)


def norm_kernel(mixed_ref, w_ref, g_ref, mlp_ref, xhat_ref, scale_ref, ga_ref, gm_ref, split_ref, context_ref, out_ref, low_ref, send_ref, sums_ref):
    attn = dot(mixed_ref[...], w_ref[...], NT)
    mlp, xhat, g = mlp_ref[...], xhat_ref[...], g_ref[...]
    both = attn * ga_ref[...] + mlp * gm_ref[...]
    inner = both - jnp.mean(both, axis=-1, keepdims=True) - xhat * jnp.mean(both * xhat, axis=-1, keepdims=True)
    new = g + scale_ref[:, :1] * inner
    out_ref[...] = new
    low_ref[...] = new.astype(BF16)
    if send_ref.shape[0] == 4:
        width = new.shape[1]
        size, rest = split_ref.shape[2], context_ref.shape[2]
        send_ref[...] = jnp.zeros_like(send_ref)
        for block in range(4):
            send_ref[block, :, :width] = new.astype(BF16)
            send_ref[block, :, width : width + size] = split_ref[block]
            send_ref[block, :, send_ref.shape[2] - rest :] = context_ref[block]
    sums_ref[...] = jnp.zeros_like(sums_ref)
    for row, value in enumerate((attn * xhat, attn, mlp * xhat, mlp, g.astype(BF16).astype(F32))):
        sums_ref[row : row + 1, :] = jnp.sum(value, axis=0, keepdims=True)


def norm_backward(g, mixed, grad_n_mlp, xhat, scale, w, split, context, send):
    rows, width = g.shape
    size = -(-split.shape[2] // 128) * 128
    sent = (4, rows, width + size + context.shape[2]) if send else (1, 8, 128)
    shapes = (shaped((rows, width), F32), shaped((rows, width), BF16), shaped(sent, BF16), shaped((8, width), F32))
    return on_chip(
        norm_kernel, shapes, "norm_back", 1_500_000_000, mixed, w["qkv"], g, grad_n_mlp, xhat, scale, w["g_attn"], w["g_mlp"], split, context
    )


def finish_kernel(unit, depth, wide_ref, up_ref, down_ref, out_ref):
    width = wide_ref.shape[1]
    for layer in range(LAYERS):
        at = layer * (unit + width)
        down_ref[layer] = wide_ref[at : at + unit, :].astype(F32)
        for block in range(4):
            row = at + unit + block * depth
            up_ref[layer, :, block * unit : (block + 1) * unit] = wide_ref[row : row + depth, :].astype(F32)
        at = LAYERS * (unit + width) + layer * depth
        out_ref[layer] = wide_ref[at : at + depth, :].astype(F32)


def finish(wide, unit, depth):
    width = wide.shape[1]
    shapes = (
        shaped((LAYERS, depth, 4 * unit), F32),
        shaped((LAYERS, unit, width), F32),
        shaped((LAYERS, depth, width), F32),
    )
    return on_chip(partial(finish_kernel, unit, depth), shapes, "finish", 5_000_000, wide)


def rotary_tables(seqs):
    device = lax.axis_index("ctx")
    devices = lax.axis_size("ctx")
    offsets = jnp.arange(BLK, dtype=jnp.int32)
    early = device * BLK + offsets
    late = 2 * BLK * devices - (device + 1) * BLK + offsets
    positions = jnp.tile(jnp.concatenate([early, late]), seqs).astype(F32)
    half = ROT // 2
    frequency = 10000.0 ** (-jnp.arange(half, dtype=F32) * 2.0 / ROT)
    angles = positions[:, None] * frequency[None, :]
    cosine, sine = lax.optimization_barrier((jnp.cos(angles), jnp.sin(angles)))
    rows = positions.shape[0]
    zero = jnp.zeros((rows, half), F32)
    rest = HEAD_DIM - ROT

    def whole(first, second, fill):
        return jnp.tile(jnp.concatenate([first, second, jnp.full((rows, rest), fill, F32)], axis=1), (1, HEADS))

    tables = (whole(cosine, cosine, 1.0), whole(zero, sine, 0.0), whole(sine, zero, 0.0))
    return lax.optimization_barrier(tables)


def cdf(value):
    return 0.5 * (1.0 + lax.erf(value * (0.5 ** 0.5)))


TN = (((0,), (0,)), ((), ()))


def split_columns(value):
    return value.reshape(value.shape[0], 4, -1).transpose(1, 0, 2)


def mlp_forward(xhat_all, w):
    n_mlp_all = (xhat_all.astype(F32) * w["g_mlp"] + w["s_mlp"]).astype(BF16)
    hidden = dot(n_mlp_all, w["up"]) + w["b_up"]
    active = (hidden * cdf(hidden)).astype(BF16)
    return n_mlp_all, hidden, active, dot(active, w["down"])


def own_sum(partial):
    rows = partial.shape[0] // 4
    return group_sum([partial[i * rows : (i + 1) * rows] for i in range(4)])


def mlp_backward(g_all, n_mlp_all, hidden, active, w):
    grad_active = dot(g_all, w["down"], NT)
    density = jnp.exp(-0.5 * hidden * hidden) * 0.3989422804014327
    grad_hidden = (grad_active * (cdf(hidden) + hidden * density)).astype(BF16)
    partial = dot(grad_hidden, w["up"], NT)
    grad_down = dot(active, g_all, TN).astype(BF16)
    grad_up = dot(n_mlp_all, grad_hidden, TN).astype(BF16)
    grad_b_up = jnp.sum(grad_hidden.astype(F32), axis=0)
    return partial, grad_down, grad_up.reshape(4, -1, grad_up.shape[1]), grad_b_up


def small_sums(sums, mixed_sums):
    width = sums.shape[1]
    bias = jnp.concatenate([mixed_sums[0, :width], mixed_sums[0, 2 * width :]])
    rest = sums[:5].reshape(5, 4, -1).transpose(1, 0, 2).reshape(4, -1)
    return jnp.concatenate([rest, bias.reshape(4, -1)], axis=1)


def gather_small(stacked):
    names = ("g_attn", "s_attn", "g_mlp", "s_mlp", "b_qv", "b_out", "b_down")
    flat = jnp.concatenate([stacked[name] for name in names], axis=1)
    every = spread(flat, "wt").astype(F32)
    found, at = {}, 0
    for name in names:
        size = stacked[name].shape[1]
        found[name] = every[:, :, at : at + size].transpose(1, 0, 2).reshape(LAYERS, -1)
        at += size
    return found


def local(tokens_in, cotangent, ln_gain_attn, ln_shift_attn, ln_gain_mlp, ln_shift_mlp, w_qkv, b_qv, w_out, b_out, w_up, b_up, w_down, b_down):
    seqs = tokens_in.shape[0]
    width = tokens_in.shape[3]
    rows = seqs * 2 * BLK
    devices = lax.axis_size("ctx")
    depth = width // 4
    unit = b_up.shape[1]
    tables = rotary_tables(seqs)
    small = gather_small(
        {"g_attn": ln_gain_attn, "s_attn": ln_shift_attn, "g_mlp": ln_gain_mlp, "s_mlp": ln_shift_mlp, "b_qv": b_qv, "b_out": b_out, "b_down": b_down}
    )
    half1 = gather_half(w_qkv[0])
    out_both = lax.all_gather(after(w_out, half1), "wt", axis=1, tiled=True)
    layers = []
    for layer in range(LAYERS):
        w = {name: small[name][layer][None] for name in small}
        w["b_q"] = w["b_qv"][:, :width]
        w["b_v"] = w["b_qv"][:, width:]
        w["out"] = out_both[layer]
        w["down"] = w_down[layer]
        w["b_up"] = b_up[layer].astype(F32)[None]
        layers.append(w)
    first, second = layers
    first["qkv"] = gather_rest(half1)
    g2 = cotangent.reshape(rows, width)
    x1 = tokens_in.reshape(rows, width).astype(F32)
    xhat1, send1, scale1, packed1 = mix(x1, first, tables, jnp.zeros((1, rows, 128), BF16))
    later_up, later_qkv, send1 = after((w_up, w_qkv[1], send1), packed1)
    packed1 = exchange(packed1, "ctx")
    spread1 = group_spread(send1[0, :, :width])

    def up_columns(value):
        return group_trade(jnp.stack([value[:, i * unit : (i + 1) * unit] for i in range(4)]))

    ups = up_columns(later_up[0])
    half2 = gather_half(later_qkv)
    out1, full1, lse1 = attend(packed1)
    ups, spread1, later_g2, later_up, half2 = after((ups, spread1, g2, w_up[1], half2), out1)
    out1 = exchange(out1, "ctx")
    first["up"] = place([b[None] for b in ups], 0).reshape(width, unit)
    second["up"] = place([b[None] for b in up_columns(later_up)], 0).reshape(width, unit)
    second["qkv"] = gather_rest(half2)
    xhat1_all = jnp.concatenate(spread1, axis=0)
    n_mlp1, hidden1, active1, partial1 = mlp_forward(xhat1_all, first)
    mlp1 = own_sum(partial1)
    split1, x2 = join(out1, x1, mlp1, first)
    xhat2, send2, scale2, packed2 = mix(x2, second, tables, split1)
    packed2 = exchange(jnp.concatenate([packed2, pull(g2, second)], axis=1), "ctx")
    packed2, grads2 = packed2[:, : 3 * BLK], packed2[:, 3 * BLK :]
    g2_all = jnp.concatenate(group_spread(after(later_g2, mlp1)), axis=0)
    landed2 = jnp.concatenate(group_trade(send2), axis=0)
    xhat2_all, context1_all = landed2[:, :width], landed2[:, width:]
    n_mlp2, hidden2, active2, partial2 = mlp_forward(xhat2_all, second)
    out2, full2, lse2 = attend(packed2)
    back2 = attend_back(packed2, grads2, full2, lse2, out2)
    done2 = back2
    back2 = exchange(back2, "ctx")
    back_partial2, grad_down2, grad_up2, grad_b_up2 = mlp_backward(g2_all, n_mlp2, hidden2, active2, second)
    sums = own_sum(jnp.concatenate([partial2, back_partial2], axis=1))
    mlp2, grad_n_mlp2 = sums[:, :width], sums[:, width:]
    split2, x3 = join(back2[:, 3 * BLK :], x2, mlp2, second)
    out_tokens = x3.astype(BF16).reshape(tokens_in.shape)
    mixed2, mixed2_split, mixed_sums2 = unmix(back2, tables)
    g1, g1_low, send3, sums2 = norm_backward(g2.astype(F32), mixed2, grad_n_mlp2, xhat2, scale2, second, mixed2_split, split2, True)
    grads1 = exchange(pull(g1_low, first), "ctx")
    landed3 = jnp.concatenate(group_trade(send3), axis=0)
    columns = mixed2_split.shape[2]
    g1_all, mixed2_all, context2_all = landed3[:, :width], landed3[:, width : width + columns], landed3[:, -depth:]
    back_partial1, grad_down1, grad_up1, grad_b_up1 = mlp_backward(g1_all, n_mlp1, hidden1, active1, first)
    back1 = exchange(attend_back(packed1, grads1, full1, lse1, lse1[None].astype(BF16)), "ctx")
    grad_up1 = place([b[None] for b in group_trade(grad_up1)], 0).reshape(width, unit)
    grad_out1 = dot(context1_all, g1_all, TN).astype(BF16)
    grad_out2 = dot(context2_all, g2_all, TN).astype(BF16)
    n_attn2_all = (xhat2_all.astype(F32) * second["g_attn"] + second["s_attn"]).astype(BF16)
    grad_up2 = group_trade(after(grad_up2, done2))
    grad_up2 = place([b[None] for b in grad_up2], 0).reshape(width, unit)
    ready = [grad_down1, grad_up1, grad_down2, grad_up2, grad_out1, grad_out2]
    lines = sum(v.shape[0] for v in ready)
    lines = -(-lines // (16 * devices)) * 16 * devices - lines
    ready = jnp.concatenate(ready + [jnp.zeros((lines, width), BF16)], axis=0)
    back1, ready = lax.optimization_barrier((back1, ready))
    wide = lax.psum_scatter(ready, "ctx", scatter_dimension=0, tiled=True)
    mixed1, mixed1_split, mixed_sums1 = unmix(back1, tables)
    mixed1_all = jnp.concatenate(group_trade(mixed1_split), axis=0)
    back_partial1, mixed2_all = after((back_partial1, mixed2_all), mixed1_split)
    grad_n_mlp1 = own_sum(back_partial1)
    grad_qkv2 = dot(n_attn2_all, mixed2_all, TN).astype(BF16)
    n_attn1_all = (xhat1_all.astype(F32) * first["g_attn"] + first["s_attn"]).astype(BF16)
    grad_qkv1 = dot(n_attn1_all, mixed1_all, TN).astype(BF16)
    g0, _, _, sums1 = norm_backward(g1, mixed1, grad_n_mlp1, xhat1, scale1, first, mixed2_split, split2, False)
    small1, small2 = small_sums(sums1, mixed_sums1), small_sums(sums2, mixed_sums2)
    smalls, hidden_sums = (small1, small2), (grad_b_up1, grad_b_up2)
    piece = width // devices

    def to_rows(value):
        size = value.shape[-1]
        lines = -(-size // columns)
        lines = -(-lines // 8) * 8
        padded = jnp.pad(value, ((0, 0), (0, lines * columns - size)))
        return padded.reshape(value.shape[0], lines, columns)

    tiny = to_rows(jnp.concatenate(smalls, axis=1).astype(BF16))
    both_qkv = [m.reshape(4, depth, columns) for m in (grad_qkv1, grad_qkv2)]
    moved = exchange(jnp.concatenate(both_qkv + [tiny], axis=1), "wt")
    tiny_size = small1.shape[1]
    small_sum = moved[:, 2 * depth :].astype(F32).sum(0).reshape(1, -1)[:, : LAYERS * tiny_size]
    tail = to_rows(jnp.concatenate([small_sum, *(u[None] for u in hidden_sums)], axis=1).astype(BF16))
    sent = jnp.concatenate(
        [moved[:, i * depth : (i + 1) * depth].reshape(devices, piece, columns) for i in range(LAYERS)]
        + [jnp.broadcast_to(tail, (devices,) + tail.shape[1:])],
        axis=1,
    )
    landed = exchange(sent, "ctx").astype(F32).sum(0)
    def side_by_side(blocks):
        return blocks.transpose(1, 0, 2).reshape(depth, -1)

    qkvs = spread(landed[: 2 * piece].astype(BF16), "ctx")
    wide = lax.all_gather(after(wide, landed), "ctx", axis=0, tiled=True)
    grad_up, grad_down, grad_out = finish(wide, unit, depth)
    qkvs = [side_by_side(qkvs[:, i * piece : (i + 1) * piece].reshape(4, depth, columns)) for i in range(LAYERS)]
    flat = landed[2 * piece :].reshape(-1)
    per_layer = [flat[layer * tiny_size : (layer + 1) * tiny_size] for layer in range(LAYERS)]
    grad_b_up = flat[LAYERS * tiny_size :][: LAYERS * unit].reshape(LAYERS, unit)

    def vector(index):
        return jnp.stack([v[index * depth : (index + 1) * depth] for v in per_layer])

    def both(one, two):
        return jnp.stack([one.astype(F32), two.astype(F32)])

    grad_bias = vector(4)
    grad_b_qv = jnp.stack([v[5 * depth :] for v in per_layer])
    grad_qkv = both(*qkvs)
    return (
        out_tokens,
        g0.reshape(tokens_in.shape),
        vector(0),
        vector(1),
        vector(2),
        vector(3),
        grad_qkv,
        grad_b_qv,
        grad_out,
        grad_bias,
        grad_up,
        grad_b_up,
        grad_down,
        grad_bias,
    )


def solution(mesh):
    tokens = P("wt", None, "ctx", None)
    vec, mat = P(None, "wt"), P(None, "wt", None)
    params = (vec, vec, vec, vec, mat, vec, mat, vec, mat, vec, mat, vec)
    return jax.shard_map(
        local,
        mesh=mesh,
        in_specs=(tokens, tokens) + params,
        out_specs=(tokens, tokens) + params,
        check_vma=False,
    )
```

```python
from functools import partial

import jax
import jax.numpy as jnp
from jax import lax
from jax.experimental import pallas as pl
from jax.experimental.pallas import tpu as pltpu
from jax.sharding import PartitionSpec as P

HEADS = 12
HEAD_DIM = 64
ROT = 16
LAYERS = 2
BLK = 32
EPS = 1e-05

F32 = jnp.float32
BF16 = jnp.bfloat16
NT = (((1,), (1,)), ((), ()))
NN = (((1,), (0,)), ((), ()))
TILE = 512


def dot(left, right, dims=NN):
    return lax.dot_general(left, right, dims, preferred_element_type=F32)


def exchange(chunks, axis):
    return lax.all_to_all(chunks, axis, 0, 0, tiled=True)


def pass_on(value, shift):
    count = lax.axis_size("wt")
    return lax.ppermute(value, "wt", [(i, (i + shift) % count) for i in range(count)])


def shifts():
    return (1, 3, 2)


def group_spread(value):
    landed = {0: value}
    for shift in shifts():
        landed[shift] = pass_on(value, shift)
    return [landed[shift] for shift in range(4)]


def group_sum(blocks):
    total = blocks[0]
    for shift in shifts():
        total = total + pass_on(blocks[shift].astype(BF16), (4 - shift) % 4).astype(F32)
    return total


def group_trade(chunks):
    here = lax.axis_index("wt")

    def chunk(shift):
        return lax.dynamic_index_in_dim(chunks, (here + shift) % 4, 0, keepdims=False)

    landed = {0: chunk(0)}
    for shift in shifts():
        landed[shift] = pass_on(chunk(shift), shift)
    return [landed[shift] for shift in range(4)]


def place(blocks, axis):
    here = lax.axis_index("wt")
    shape = list(blocks[0].shape)
    size = shape[axis]
    shape[axis] = 4 * size
    whole = jnp.zeros(shape, blocks[0].dtype)
    for shift in range(4):
        whole = lax.dynamic_update_slice_in_dim(whole, blocks[shift], ((here - shift) % 4) * size, axis)
    return whole


def swap(value):
    return lax.ppermute(value, "ctx", [(i, i ^ 1) for i in range(lax.axis_size("ctx"))])


def gather_half(shard):
    core = lax.axis_index("ctx") % 2
    half = shard.shape[0] // 2
    mine = lax.dynamic_slice_in_dim(shard, core * half, half, 0)
    return place([b[None] for b in group_spread(mine)], 0)


def gather_rest(here):
    core = lax.axis_index("ctx") % 2
    other = swap(here)
    first = jnp.where(core == 0, here, other)
    second = jnp.where(core == 0, other, here)
    return jnp.stack([first, second], axis=1).reshape(-1, here.shape[2])


def after(values, first):
    return lax.optimization_barrier((values, first))[0]


def spread(value, axis):
    count = lax.axis_size(axis)
    return exchange(jnp.broadcast_to(value[None], (count,) + value.shape), axis)


def tile_list(size):
    tiles = []
    for start in range(0, size, TILE):
        keys = [(0, k, k == start) for k in range(0, start + TILE, TILE)]
        tiles.append((0, start, keys))
    for start in range(0, size, TILE):
        keys = [(0, k, False) for k in range(0, size, TILE)]
        keys += [(1, k, k == start) for k in range(start, size, TILE)]
        tiles.append((1, start, keys))
    return tiles


def tile_mask(half):
    row = lax.broadcasted_iota(jnp.int32, (TILE, TILE), 0)
    col = lax.broadcasted_iota(jnp.int32, (TILE, TILE), 1)
    if half:
        shift = BLK.bit_length() - 1
        row_pos = (row & (BLK - 1)) - ((row >> shift) << shift)
        col_pos = (col & (BLK - 1)) - ((col >> shift) << shift)
        return row_pos <= col_pos
    return row <= col


def forward_kernel(in_ref, out_ref, full_ref, lse_ref, q_scr, k_scr, vt_scr):
    count = in_ref.shape[0]
    size = count * BLK
    for half in range(2):
        both = in_ref[:, half * BLK : (half + 1) * BLK, :].reshape(size, 128)
        q_scr[half] = both[:, :64] * jnp.asarray(HEAD_DIM ** -0.5, BF16)
        k_scr[half] = both[:, 64:]
    values = in_ref[:, 2 * BLK : 3 * BLK, :].reshape(size, 128)
    vt_scr[...] = values.astype(F32).T.astype(BF16)
    for half, start, keys in tile_list(size):
        query = q_scr[half, start : start + TILE, :]
        top = jnp.full((1, TILE), -1e30, F32)
        total = jnp.zeros((1, TILE), F32)
        acc = jnp.zeros((64, TILE), F32)
        for key_half, key_start, masked in keys:
            key = k_scr[key_half, key_start : key_start + TILE, :]
            scores = dot(key, query, NT)
            if masked:
                scores = jnp.where(tile_mask(half), scores, -1e30)
            new_top = jnp.maximum(top, jnp.max(scores, axis=0, keepdims=True))
            raised = jnp.exp(scores - new_top)
            keep = jnp.exp(top - new_top)
            total = total * keep + jnp.sum(raised, axis=0, keepdims=True)
            value = vt_scr[key_half * 64 : (key_half + 1) * 64, key_start : key_start + TILE]
            acc = acc * keep + dot(value, raised.astype(BF16))
            top = new_top
        full_ref[half * 64 : (half + 1) * 64, start : start + TILE] = acc / total
        lse_ref[half : half + 1, start : start + TILE] = top + jnp.log(total)
    out_ref[...] = full_ref[...].T.astype(BF16).reshape(count, BLK, 128)


def backward_kernel(in_ref, grad_ref, full_ref, lse_ref, carry_ref, out_ref, q_scr, k_scr, kt_scr, v_scr, do_scr, delta_scr, dq_scr, dk_scr, dv_scr):
    count = in_ref.shape[0]
    size = count * BLK
    grads = grad_ref[...].reshape(size, 128)
    grads_t = grads.astype(F32).T
    product = grads_t * full_ref[...]
    values = in_ref[:, 2 * BLK : 3 * BLK, :].reshape(size, 128)
    for half in range(2):
        both = in_ref[:, half * BLK : (half + 1) * BLK, :].reshape(size, 128)
        q_scr[half] = both[:, :64] * jnp.asarray(HEAD_DIM ** -0.5, BF16)
        k_scr[half] = both[:, 64:]
        kt_scr[half] = both.astype(F32).T[64:, :].astype(BF16)
        lanes = slice(half * 64, (half + 1) * 64)
        v_scr[half] = values[:, lanes]
        do_scr[half] = grads[:, lanes]
        delta_scr[half : half + 1, :] = jnp.sum(product[lanes, :], axis=0, keepdims=True)
    dk_scr[...] = jnp.zeros_like(dk_scr)
    dv_scr[...] = jnp.zeros_like(dv_scr)
    for half, start, keys in tile_list(size):
        rows = slice(start, start + TILE)
        query = q_scr[half, rows, :]
        grad = do_scr[half, rows, :]
        lse = lse_ref[half : half + 1, rows]
        delta = delta_scr[half : half + 1, rows]
        acc = jnp.zeros((64, TILE), F32)
        for key_half, key_start, masked in keys:
            key_rows = slice(key_start, key_start + TILE)
            scores = dot(k_scr[key_half, key_rows, :], query, NT)
            if masked:
                scores = jnp.where(tile_mask(half), scores, -1e30)
            probs = jnp.exp(scores - lse)
            grad_probs = dot(v_scr[key_half, key_rows, :], grad, NT)
            grad_scores = (probs * (grad_probs - delta)).astype(BF16)
            dv_scr[key_half, key_rows, :] += dot(probs.astype(BF16), grad)
            dk_scr[key_half, key_rows, :] += dot(grad_scores, query)
            acc += dot(kt_scr[key_half, :, key_rows], grad_scores)
        dq_scr[half * 64 : (half + 1) * 64, rows] = acc * (HEAD_DIM ** -0.5)
    queries = dq_scr[...].T
    for half in range(2):
        both = jnp.concatenate([queries[:, half * 64 : (half + 1) * 64], dk_scr[half]], axis=1)
        out_ref[:, half * BLK : (half + 1) * BLK, :] = both.astype(BF16).reshape(count, BLK, 128)
    if carry_ref.shape[1] > 8:
        out_ref[:, 3 * BLK :, :] = carry_ref[...]
    both = jnp.concatenate([dv_scr[0], dv_scr[1]], axis=1)
    out_ref[:, 2 * BLK : 3 * BLK, :] = both.astype(BF16).reshape(count, BLK, 128)


def attend(packed):
    count = packed.shape[0]
    size = count * BLK
    return pl.pallas_call(
        forward_kernel,
        out_shape=(
            jax.ShapeDtypeStruct((count, BLK, 128), BF16),
            jax.ShapeDtypeStruct((128, size), F32),
            jax.ShapeDtypeStruct((8, size), F32),
        ),
        in_specs=[pl.BlockSpec(memory_space=pltpu.VMEM)],
        out_specs=[pl.BlockSpec(memory_space=pltpu.VMEM)] * 3,
        scratch_shapes=[
            pltpu.VMEM((2, size, 64), BF16),
            pltpu.VMEM((2, size, 64), BF16),
            pltpu.VMEM((128, size), BF16),
        ],
        compiler_params=pltpu.CompilerParams(vmem_limit_bytes=48 << 20),
        cost_estimate=pl.CostEstimate(flops=20_000_000_000, bytes_accessed=20_000_000, transcendentals=2_600_000),
        name="attend",
    )(packed)


def attend_back(packed, grads, full, lse, carry):
    extra = carry.shape[1] if carry.shape[1] > 8 else 0
    count = packed.shape[0]
    size = count * BLK
    return pl.pallas_call(
        backward_kernel,
        out_shape=jax.ShapeDtypeStruct((count, 3 * BLK + extra, 128), BF16),
        in_specs=[pl.BlockSpec(memory_space=pltpu.VMEM)] * 5,
        out_specs=pl.BlockSpec(memory_space=pltpu.VMEM),
        scratch_shapes=[
            pltpu.VMEM((2, size, 64), BF16),
            pltpu.VMEM((2, size, 64), BF16),
            pltpu.VMEM((2, 64, size), BF16),
            pltpu.VMEM((2, size, 64), BF16),
            pltpu.VMEM((2, size, 64), BF16),
            pltpu.VMEM((8, size), F32),
            pltpu.VMEM((128, size), F32),
            pltpu.VMEM((2, size, 64), F32),
            pltpu.VMEM((2, size, 64), F32),
        ],
        compiler_params=pltpu.CompilerParams(vmem_limit_bytes=48 << 20),
        cost_estimate=pl.CostEstimate(flops=40_000_000_000, bytes_accessed=40_000_000, transcendentals=2_600_000),
        name="attend_back",
    )(packed, grads, full, lse, carry)


def kernel_turn(value, tables, sign):
    cosine, up, down = tables
    half = ROT // 2
    back = value.shape[1] - half
    turned = pltpu.roll(value, half, 1) * up - pltpu.roll(value, back, 1) * down
    return value * cosine + sign * turned


def head(value, rows, index):
    return value[rows, index * HEAD_DIM : (index + 1) * HEAD_DIM]


def mix_kernel(x_ref, gain_ref, shift_ref, w_ref, bq_ref, bv_ref, cos_ref, up_ref, down_ref, extra_ref, xhat_ref, send_ref, scale_ref, out_ref):
    x = x_ref[...]
    rows, width = x.shape
    centred = x - jnp.mean(x, axis=-1, keepdims=True)
    scale = lax.rsqrt(jnp.mean(centred * centred, axis=-1, keepdims=True) + EPS)
    xhat = centred * scale
    xhat_ref[...] = xhat
    for block in range(send_ref.shape[0]):
        send_ref[block, :, :width] = xhat.astype(BF16)
        send_ref[block, :, width:] = extra_ref[block]
    scale_ref[...] = jnp.broadcast_to(scale, scale_ref.shape)
    normed = (xhat * gain_ref[...] + shift_ref[...]).astype(BF16)
    tables = (cos_ref[...], up_ref[...], down_ref[...])
    query = kernel_turn(dot(normed, w_ref[:, :width]) + bq_ref[...], tables, 1.0)
    key = kernel_turn(dot(normed, w_ref[:, width : 2 * width]), tables, 1.0)
    value = dot(normed, w_ref[:, 2 * width :]) + bv_ref[...]
    seqs = rows // (2 * BLK)
    for s in range(seqs):
        at = s * 2 * BLK
        whole, early, late = slice(at, at + 2 * BLK), slice(at, at + BLK), slice(at + BLK, at + 2 * BLK)
        for h in range(HEADS):
            pair = jnp.concatenate([head(query, whole, h), head(key, whole, h)], axis=1)
            out_ref[s * HEADS + h, : 2 * BLK, :] = pair.astype(BF16)
            pair = jnp.concatenate([head(value, early, h), head(value, late, h)], axis=1)
            out_ref[s * HEADS + h, 2 * BLK :, :] = pair.astype(BF16)
    spare = out_ref.shape[0] - seqs * HEADS
    out_ref[seqs * HEADS :, :, :] = jnp.zeros((spare,) + out_ref.shape[1:], BF16)


def on_chip(kernel, out_shape, name, flops, *operands, scratch=()):
    many = isinstance(out_shape, tuple)
    spec = pl.BlockSpec(memory_space=pltpu.VMEM)
    return pl.pallas_call(
        kernel,
        out_shape=out_shape,
        in_specs=[spec] * len(operands),
        out_specs=[spec] * len(out_shape) if many else spec,
        scratch_shapes=list(scratch),
        compiler_params=pltpu.CompilerParams(vmem_limit_bytes=48 << 20),
        cost_estimate=pl.CostEstimate(flops=flops, bytes_accessed=8_000_000, transcendentals=0),
        name=name,
    )(*operands)


def shaped(shape, dtype):
    return jax.ShapeDtypeStruct(shape, dtype)


def mix(x, w, tables, extra):
    rows, width = x.shape
    count = lax.axis_size("ctx")
    shapes = (
        shaped((rows, width), F32),
        shaped((extra.shape[0], rows, width + extra.shape[2]), BF16),
        shaped((rows, 128), F32),
        shaped((count, 3 * BLK, 128), BF16),
    )
    return on_chip(mix_kernel, shapes, "mix", 5_000_000_000, x, w["g_attn"], w["s_attn"], w["qkv"], w["b_q"], w["b_v"], *tables, extra)


def join_kernel(tile_ref, x_ref, mlp_ref, w_ref, bias_ref, split_ref, out_ref, context):
    rows, width = context.shape
    for s in range(rows // (2 * BLK)):
        for half in range(2):
            at = (2 * s + half) * BLK
            lanes = slice(half * HEAD_DIM, (half + 1) * HEAD_DIM)
            row = [tile_ref[s * HEADS + h, :, lanes] for h in range(HEADS)]
            context[at : at + BLK, :] = jnp.concatenate(row, axis=1)
    size = width // 4
    for block in range(4):
        split_ref[block] = context[:, block * size : (block + 1) * size]
    out_ref[...] = x_ref[...] + dot(context[...], w_ref[...]) + (mlp_ref[...] + bias_ref[...])


def join(tiles, x, mlp, w):
    rows, width = x.shape
    shapes = (shaped((4, rows, width // 4), BF16), shaped((rows, width), F32))
    scratch = [pltpu.VMEM((rows, width), BF16)]
    return on_chip(join_kernel, shapes, "join", 500_000_000, tiles, x, mlp, w["out"], w["b_out"] + w["b_down"], scratch=scratch)


def pull_kernel(g_ref, w_ref, out_ref):
    grad = dot(g_ref[...], w_ref[...], NT)
    seqs = grad.shape[0] // (2 * BLK)
    for s in range(seqs):
        at = s * 2 * BLK
        for h in range(HEADS):
            early, late = head(grad, slice(at, at + BLK), h), head(grad, slice(at + BLK, at + 2 * BLK), h)
            out_ref[s * HEADS + h] = jnp.concatenate([early, late], axis=1).astype(BF16)
    spare = out_ref.shape[0] - seqs * HEADS
    out_ref[seqs * HEADS :, :, :] = jnp.zeros((spare,) + out_ref.shape[1:], BF16)


def pull(g_low, w):
    count = lax.axis_size("ctx")
    return on_chip(pull_kernel, shaped((count, BLK, 128), BF16), "pull", 500_000_000, g_low, w["out"])


def unmix_kernel(tile_ref, cos_ref, up_ref, down_ref, mixed_ref, split_ref, sums_ref):
    rows, width = cos_ref.shape
    tables = (cos_ref[...], up_ref[...], down_ref[...])
    parts = [[], [], []]
    for s in range(rows // (2 * BLK)):
        for part in range(2):
            lanes = slice(part * HEAD_DIM, (part + 1) * HEAD_DIM)
            row = [tile_ref[s * HEADS + h, : 2 * BLK, lanes] for h in range(HEADS)]
            parts[part].append(jnp.concatenate(row, axis=1))
        for half in range(2):
            lanes = slice(half * HEAD_DIM, (half + 1) * HEAD_DIM)
            row = [tile_ref[s * HEADS + h, 2 * BLK : 3 * BLK, lanes] for h in range(HEADS)]
            parts[2].append(jnp.concatenate(row, axis=1))
    query, key, value = (jnp.concatenate(part, axis=0) for part in parts)
    mixed_ref[:, :width] = kernel_turn(query.astype(F32), tables, -1.0).astype(BF16)
    mixed_ref[:, width : 2 * width] = kernel_turn(key.astype(F32), tables, -1.0).astype(BF16)
    mixed_ref[:, 2 * width :] = value
    size = 3 * width // 4
    for block in range(4):
        split_ref[block] = mixed_ref[:, block * size : (block + 1) * size]
    sums_ref[...] = jnp.sum(mixed_ref[...].astype(F32), axis=0, keepdims=True)


def unmix(tiles, tables):
    rows, width = tables[0].shape
    shapes = (
        shaped((rows, 3 * width), BF16),
        shaped((4, rows, 3 * width // 4), BF16),
        shaped((1, 3 * width), F32),
    )
    return on_chip(unmix_kernel, shapes, "unmix", 500_000_000, tiles, *tables)


def norm_kernel(mixed_ref, w_ref, g_ref, mlp_ref, xhat_ref, scale_ref, ga_ref, gm_ref, split_ref, context_ref, out_ref, low_ref, send_ref, sums_ref):
    attn = dot(mixed_ref[...], w_ref[...], NT)
    mlp, xhat, g = mlp_ref[...], xhat_ref[...], g_ref[...]
    both = attn * ga_ref[...] + mlp * gm_ref[...]
    inner = both - jnp.mean(both, axis=-1, keepdims=True) - xhat * jnp.mean(both * xhat, axis=-1, keepdims=True)
    new = g + scale_ref[:, :1] * inner
    out_ref[...] = new
    low_ref[...] = new.astype(BF16)
    if send_ref.shape[0] == 4:
        width = new.shape[1]
        size, rest = split_ref.shape[2], context_ref.shape[2]
        send_ref[...] = jnp.zeros_like(send_ref)
        for block in range(4):
            send_ref[block, :, :width] = new.astype(BF16)
            send_ref[block, :, width : width + size] = split_ref[block]
            send_ref[block, :, send_ref.shape[2] - rest :] = context_ref[block]
    sums_ref[...] = jnp.zeros_like(sums_ref)
    for row, value in enumerate((attn * xhat, attn, mlp * xhat, mlp, g.astype(BF16).astype(F32))):
        sums_ref[row : row + 1, :] = jnp.sum(value, axis=0, keepdims=True)


def norm_backward(g, mixed, grad_n_mlp, xhat, scale, w, split, context, send):
    rows, width = g.shape
    size = -(-split.shape[2] // 128) * 128
    sent = (4, rows, width + size + context.shape[2]) if send else (1, 8, 128)
    shapes = (shaped((rows, width), F32), shaped((rows, width), BF16), shaped(sent, BF16), shaped((8, width), F32))
    return on_chip(
        norm_kernel, shapes, "norm_back", 1_500_000_000, mixed, w["qkv"], g, grad_n_mlp, xhat, scale, w["g_attn"], w["g_mlp"], split, context
    )


def finish_kernel(unit, depth, wide_ref, up_ref, down_ref, out_ref):
    width = wide_ref.shape[1]
    for layer in range(LAYERS):
        at = layer * (unit + width)
        down_ref[layer] = wide_ref[at : at + unit, :].astype(F32)
        for block in range(4):
            row = at + unit + block * depth
            up_ref[layer, :, block * unit : (block + 1) * unit] = wide_ref[row : row + depth, :].astype(F32)
        at = LAYERS * (unit + width) + layer * depth
        out_ref[layer] = wide_ref[at : at + depth, :].astype(F32)


def finish(wide, unit, depth):
    width = wide.shape[1]
    shapes = (
        shaped((LAYERS, depth, 4 * unit), F32),
        shaped((LAYERS, unit, width), F32),
        shaped((LAYERS, depth, width), F32),
    )
    return on_chip(partial(finish_kernel, unit, depth), shapes, "finish", 5_000_000, wide)


def rotary_tables(seqs):
    device = lax.axis_index("ctx")
    devices = lax.axis_size("ctx")
    offsets = jnp.arange(BLK, dtype=jnp.int32)
    early = device * BLK + offsets
    late = 2 * BLK * devices - (device + 1) * BLK + offsets
    positions = jnp.tile(jnp.concatenate([early, late]), seqs).astype(F32)
    half = ROT // 2
    frequency = 10000.0 ** (-jnp.arange(half, dtype=F32) * 2.0 / ROT)
    angles = positions[:, None] * frequency[None, :]
    cosine, sine = lax.optimization_barrier((jnp.cos(angles), jnp.sin(angles)))
    rows = positions.shape[0]
    zero = jnp.zeros((rows, half), F32)
    rest = HEAD_DIM - ROT

    def whole(first, second, fill):
        return jnp.tile(jnp.concatenate([first, second, jnp.full((rows, rest), fill, F32)], axis=1), (1, HEADS))

    tables = (whole(cosine, cosine, 1.0), whole(zero, sine, 0.0), whole(sine, zero, 0.0))
    return lax.optimization_barrier(tables)


def cdf(value):
    return 0.5 * (1.0 + lax.erf(value * (0.5 ** 0.5)))


TN = (((0,), (0,)), ((), ()))


def split_columns(value):
    return value.reshape(value.shape[0], 4, -1).transpose(1, 0, 2)


def mlp_forward(xhat_all, w):
    n_mlp_all = (xhat_all.astype(F32) * w["g_mlp"] + w["s_mlp"]).astype(BF16)
    hidden = dot(n_mlp_all, w["up"]) + w["b_up"]
    active = (hidden * cdf(hidden)).astype(BF16)
    return n_mlp_all, hidden, active, dot(active, w["down"])


def own_sum(partial):
    rows = partial.shape[0] // 4
    return group_sum([partial[i * rows : (i + 1) * rows] for i in range(4)])


def mlp_backward(g_all, n_mlp_all, hidden, active, w):
    grad_active = dot(g_all, w["down"], NT)
    density = jnp.exp(-0.5 * hidden * hidden) * 0.3989422804014327
    grad_hidden = (grad_active * (cdf(hidden) + hidden * density)).astype(BF16)
    partial = dot(grad_hidden, w["up"], NT)
    grad_down = dot(active, g_all, TN).astype(BF16)
    grad_up = dot(n_mlp_all, grad_hidden, TN).astype(BF16)
    grad_b_up = jnp.sum(grad_hidden.astype(F32), axis=0)
    return partial, grad_down, grad_up.reshape(4, -1, grad_up.shape[1]), grad_b_up


def small_sums(sums, mixed_sums):
    width = sums.shape[1]
    bias = jnp.concatenate([mixed_sums[0, :width], mixed_sums[0, 2 * width :]])
    rest = sums[:5].reshape(5, 4, -1).transpose(1, 0, 2).reshape(4, -1)
    return jnp.concatenate([rest, bias.reshape(4, -1)], axis=1)


def gather_small(stacked):
    names = ("g_attn", "s_attn", "g_mlp", "s_mlp", "b_qv", "b_out", "b_down")
    flat = jnp.concatenate([stacked[name] for name in names], axis=1)
    every = spread(flat, "wt").astype(F32)
    found, at = {}, 0
    for name in names:
        size = stacked[name].shape[1]
        found[name] = every[:, :, at : at + size].transpose(1, 0, 2).reshape(LAYERS, -1)
        at += size
    return found


def local(tokens_in, cotangent, ln_gain_attn, ln_shift_attn, ln_gain_mlp, ln_shift_mlp, w_qkv, b_qv, w_out, b_out, w_up, b_up, w_down, b_down):
    seqs = tokens_in.shape[0]
    width = tokens_in.shape[3]
    rows = seqs * 2 * BLK
    devices = lax.axis_size("ctx")
    depth = width // 4
    unit = b_up.shape[1]
    tables = rotary_tables(seqs)
    small = gather_small(
        {"g_attn": ln_gain_attn, "s_attn": ln_shift_attn, "g_mlp": ln_gain_mlp, "s_mlp": ln_shift_mlp, "b_qv": b_qv, "b_out": b_out, "b_down": b_down}
    )
    half1 = gather_half(w_qkv[0])
    out_both = lax.all_gather(after(w_out, half1), "wt", axis=1, tiled=True)
    layers = []
    for layer in range(LAYERS):
        w = {name: small[name][layer][None] for name in small}
        w["b_q"] = w["b_qv"][:, :width]
        w["b_v"] = w["b_qv"][:, width:]
        w["out"] = out_both[layer]
        w["down"] = w_down[layer]
        w["b_up"] = b_up[layer].astype(F32)[None]
        layers.append(w)
    first, second = layers
    first["qkv"] = gather_rest(half1)
    g2 = cotangent.reshape(rows, width)
    x1 = tokens_in.reshape(rows, width).astype(F32)
    xhat1, send1, scale1, packed1 = mix(x1, first, tables, jnp.zeros((1, rows, 128), BF16))
    later_up, send1 = after((w_up, send1), packed1)
    packed1 = exchange(packed1, "ctx")
    spread1 = group_spread(send1[0, :, :width])

    def up_columns(value):
        return group_trade(jnp.stack([value[:, i * unit : (i + 1) * unit] for i in range(4)]))

    ups = up_columns(later_up[0])
    out1, full1, lse1 = attend(packed1)
    ups, spread1, later_g2, later_up, later_qkv = after((ups, spread1, g2, w_up[1], w_qkv[1]), out1)
    half2 = gather_half(later_qkv)
    out1 = exchange(out1, "ctx")
    first["up"] = place([b[None] for b in ups], 0).reshape(width, unit)
    second["up"] = place([b[None] for b in up_columns(later_up)], 0).reshape(width, unit)
    second["qkv"] = gather_rest(half2)
    xhat1_all = jnp.concatenate(spread1, axis=0)
    n_mlp1, hidden1, active1, partial1 = mlp_forward(xhat1_all, first)
    mlp1 = own_sum(partial1)
    split1, x2 = join(out1, x1, mlp1, first)
    xhat2, send2, scale2, packed2 = mix(x2, second, tables, split1)
    packed2 = exchange(jnp.concatenate([packed2, pull(g2, second)], axis=1), "ctx")
    packed2, grads2 = packed2[:, : 3 * BLK], packed2[:, 3 * BLK :]
    g2_all = jnp.concatenate(group_spread(after(later_g2, mlp1)), axis=0)
    landed2 = jnp.concatenate(group_trade(send2), axis=0)
    xhat2_all, context1_all = landed2[:, :width], landed2[:, width:]
    n_mlp2, hidden2, active2, partial2 = mlp_forward(xhat2_all, second)
    out2, full2, lse2 = attend(packed2)
    back2 = attend_back(packed2, grads2, full2, lse2, out2)
    done2 = back2
    back2 = exchange(back2, "ctx")
    back_partial2, grad_down2, grad_up2, grad_b_up2 = mlp_backward(g2_all, n_mlp2, hidden2, active2, second)
    sums = own_sum(jnp.concatenate([partial2, back_partial2], axis=1))
    mlp2, grad_n_mlp2 = sums[:, :width], sums[:, width:]
    split2, x3 = join(back2[:, 3 * BLK :], x2, mlp2, second)
    out_tokens = x3.astype(BF16).reshape(tokens_in.shape)
    mixed2, mixed2_split, mixed_sums2 = unmix(back2, tables)
    g1, g1_low, send3, sums2 = norm_backward(g2.astype(F32), mixed2, grad_n_mlp2, xhat2, scale2, second, mixed2_split, split2, True)
    grads1 = exchange(pull(g1_low, first), "ctx")
    landed3 = jnp.concatenate(group_trade(send3), axis=0)
    columns = mixed2_split.shape[2]
    g1_all, mixed2_all, context2_all = landed3[:, :width], landed3[:, width : width + columns], landed3[:, -depth:]
    back_partial1, grad_down1, grad_up1, grad_b_up1 = mlp_backward(g1_all, n_mlp1, hidden1, active1, first)
    back1 = exchange(attend_back(packed1, grads1, full1, lse1, lse1[None].astype(BF16)), "ctx")
    grad_up1 = place([b[None] for b in group_trade(grad_up1)], 0).reshape(width, unit)
    grad_out1 = dot(context1_all, g1_all, TN).astype(BF16)
    grad_out2 = dot(context2_all, g2_all, TN).astype(BF16)
    n_attn2_all = (xhat2_all.astype(F32) * second["g_attn"] + second["s_attn"]).astype(BF16)
    grad_up2 = group_trade(after(grad_up2, done2))
    grad_up2 = place([b[None] for b in grad_up2], 0).reshape(width, unit)
    ready = [grad_down1, grad_up1, grad_down2, grad_up2, grad_out1, grad_out2]
    lines = sum(v.shape[0] for v in ready)
    lines = -(-lines // (16 * devices)) * 16 * devices - lines
    ready = jnp.concatenate(ready + [jnp.zeros((lines, width), BF16)], axis=0)
    back1, ready = lax.optimization_barrier((back1, ready))
    wide = lax.psum_scatter(ready, "ctx", scatter_dimension=0, tiled=True)
    mixed1, mixed1_split, mixed_sums1 = unmix(back1, tables)
    mixed1_all = jnp.concatenate(group_trade(mixed1_split), axis=0)
    back_partial1, mixed2_all = after((back_partial1, mixed2_all), mixed1_split)
    grad_n_mlp1 = own_sum(back_partial1)
    grad_qkv2 = dot(n_attn2_all, mixed2_all, TN).astype(BF16)
    n_attn1_all = (xhat1_all.astype(F32) * first["g_attn"] + first["s_attn"]).astype(BF16)
    grad_qkv1 = dot(n_attn1_all, mixed1_all, TN).astype(BF16)
    g0, _, _, sums1 = norm_backward(g1, mixed1, grad_n_mlp1, xhat1, scale1, first, mixed2_split, split2, False)
    small1, small2 = small_sums(sums1, mixed_sums1), small_sums(sums2, mixed_sums2)
    smalls, hidden_sums = (small1, small2), (grad_b_up1, grad_b_up2)
    piece = width // devices

    def to_rows(value):
        size = value.shape[-1]
        lines = -(-size // columns)
        lines = -(-lines // 8) * 8
        padded = jnp.pad(value, ((0, 0), (0, lines * columns - size)))
        return padded.reshape(value.shape[0], lines, columns)

    tiny = to_rows(jnp.concatenate(smalls, axis=1).astype(BF16))
    both_qkv = [m.reshape(4, depth, columns) for m in (grad_qkv1, grad_qkv2)]
    moved = exchange(jnp.concatenate(both_qkv + [tiny], axis=1), "wt")
    tiny_size = small1.shape[1]
    small_sum = moved[:, 2 * depth :].astype(F32).sum(0).reshape(1, -1)[:, : LAYERS * tiny_size]
    tail = to_rows(jnp.concatenate([small_sum, *(u[None] for u in hidden_sums)], axis=1).astype(BF16))
    sent = jnp.concatenate(
        [moved[:, i * depth : (i + 1) * depth].reshape(devices, piece, columns) for i in range(LAYERS)]
        + [jnp.broadcast_to(tail, (devices,) + tail.shape[1:])],
        axis=1,
    )
    landed = exchange(sent, "ctx").astype(F32).sum(0)
    def side_by_side(blocks):
        return blocks.transpose(1, 0, 2).reshape(depth, -1)

    qkvs = spread(landed[: 2 * piece].astype(BF16), "ctx")
    wide = lax.all_gather(after(wide, landed), "ctx", axis=0, tiled=True)
    grad_up, grad_down, grad_out = finish(wide, unit, depth)
    qkvs = [side_by_side(qkvs[:, i * piece : (i + 1) * piece].reshape(4, depth, columns)) for i in range(LAYERS)]
    flat = landed[2 * piece :].reshape(-1)
    per_layer = [flat[layer * tiny_size : (layer + 1) * tiny_size] for layer in range(LAYERS)]
    grad_b_up = flat[LAYERS * tiny_size :][: LAYERS * unit].reshape(LAYERS, unit)

    def vector(index):
        return jnp.stack([v[index * depth : (index + 1) * depth] for v in per_layer])

    def both(one, two):
        return jnp.stack([one.astype(F32), two.astype(F32)])

    grad_bias = vector(4)
    grad_b_qv = jnp.stack([v[5 * depth :] for v in per_layer])
    grad_qkv = both(*qkvs)
    return (
        out_tokens,
        g0.reshape(tokens_in.shape),
        vector(0),
        vector(1),
        vector(2),
        vector(3),
        grad_qkv,
        grad_b_qv,
        grad_out,
        grad_bias,
        grad_up,
        grad_b_up,
        grad_down,
        grad_bias,
    )


def solution(mesh):
    tokens = P("wt", None, "ctx", None)
    vec, mat = P(None, "wt"), P(None, "wt", None)
    params = (vec, vec, vec, vec, mat, vec, mat, vec, mat, vec, mat, vec)
    return jax.shard_map(
        local,
        mesh=mesh,
        in_specs=(tokens, tokens) + params,
        out_specs=(tokens, tokens) + params,
        check_vma=False,
    )
```
